256 devices in a mesh: gx: 16 (over y_lo, x, core), gy: 8 (over z), gz: 2 (over y_hi).
Axes of the slice: x: 4, y: 4 (y_hi: 2, y_lo: 2; y = y_hi * 2 + y_lo), z: 8, core: 2. Of those that a mesh axis runs over, the one named last changes fastest.
Arguments:
- e_field: float32 [3, 128, 128, 256], P(None, 'gx', 'gy', 'gz'), may hold values from -6 to 6
- h_field: float32 [3, 128, 128, 256], P(None, 'gx', 'gy', 'gz'), may hold values from -6 to 6
- permittivity: float32 [128, 128, 256], P('gx', 'gy', 'gz'), may hold values from 1 to 4
- wall_mask: int32 [128, 128, 256], P('gx', 'gy', 'gz'), may hold values 0 or 1
- poles: float32 [8, 3, 128, 128, 256], P(None, None, 'gx', 'gy', 'gz'), may hold values from -4 to 4
- pole_decay: float32 [8], replicated, may hold values from 0.2 to 0.95
- pole_gain: float32 [8], replicated, may hold values from 0.05 to 0.3
- face_cells: int32 [8192], P(('gx', 'gy', 'gz')), may hold values from 0 to 16383
- owners: int32 [8192, 1], P(('gx', 'gy', 'gz')), may hold values from 0 to 15; in each aligned block of 32 rows (0 to 31, 32 to 63, ...) at most 4 rows name the same one
- history: bfloat16 [63, 4, 8192], P(None, None, ('gx', 'gy', 'gz')), may hold values from -6 to 6
- steering: bfloat16 [4, 16384, 4096], P(None, ('gx', 'gy'), 'gz'), may hold values from -0.03125 to 0.03125
Outputs:
- e_next: float32 [3, 128, 128, 256], P(None, 'gx', 'gy', 'gz')
- h_next: float32 [3, 128, 128, 256], P(None, 'gx', 'gy', 'gz')
- poles_next: float32 [8, 3, 128, 128, 256], P(None, None, 'gx', 'gy', 'gz')
- far_field: float32 [2, 256, 4096], P(None, ('gx', 'gy'), 'gz')
The draws below stay inside these ranges and needn't reach their ends.
Inputs may be any that keep to these rules, and one draw needn't show every extreme that they name: `face_cells`: index of the sample's cell within its device's block, row-major over 8 x 16 x 128. `owners`: among the samples of one device at most 4 name the same owner, and some device has exactly 4 for one owner.
All inputs are finite; a program needn't handle non-finite values. No bound on the sum of `wall_mask` on one device may be relied on, other than what follows from the above.
Results may differ from the reference program's by a relative error of at most 0.00063.
Values may be sent and summed in bfloat16 or wider, within the bound.
No kernel may reach another device: no remote copies, remote signals or barrier semaphores. Data moves between devices by JAX's collectives and lax.ppermute only.
A program may use at most 64 MiB of HBM per device.

```python
import math
import jax
import jax.numpy as jnp
import numpy as np
from jax import lax

CX = 8
CY = 16
CZ = 128
K_DEV = 32
POLES = 8
STEPS = 64
FREQS = 256
DIRS = 4096
NX = 128
NY = 128
NZ = 256
FACES = 8192
CAP = 4
TILE = 128
ROWS = 16384
N_GX = 16
N_GY = 8
N_GZ = 2


def plant(drawn, rng, smallest, high):
    dims = drawn.shape
    place = [jax.random.randint(jax.random.fold_in(rng, axis), (), 0, dims[axis]) for axis in range(len(dims))]
    drawn = drawn.at[tuple(place)].set(smallest)
    longest = dims.index(max(dims))
    place[longest] = (place[longest] + 1) % dims[longest]
    return drawn.at[tuple(place)].set(high)


def block_scale(key, dims, cuts, low, high):
    def one(position, blocks):
        draws = jax.random.uniform(jax.random.fold_in(jax.random.fold_in(key, 6), position), (blocks,), jnp.float32, low / len(cuts), high / len(cuts))
        return jnp.repeat(jnp.exp(draws), dims[position] // blocks).reshape((-1,) + (1,) * (len(dims) - position - 1))

    factor_of = one(*cuts[0])
    for cut in cuts[1:]:
        factor_of = factor_of * one(*cut)
    return factor_of


def shared_out(stream_key, own, number, rows, amount, top, most, lean):
    ranking = jax.random.permutation(stream_key, amount)
    packed, common = load_shares(amount, rows * top, most, lean, True), load_shares(amount, rows * top, most, lean, False)
    places = jnp.arange(amount)

    def named(sizes, rotation):
        used = int((sizes > 0).sum())
        fixed = max(1, used // 4)
        passed = fixed + (places - fixed + rotation * (used - fixed)) % max(1, amount - fixed)
        return jnp.zeros((amount,), jnp.int32).at[ranking[jnp.where(places < fixed, places, passed)]].set(jnp.asarray(sizes, jnp.int32))

    sizes = jnp.where(number % 4 == 0, named(packed, number // 4), named(common, number - number // 4 - 1))
    mixed = jax.random.permutation(jax.random.fold_in(own, 3), amount)
    giver, sink = mixed[0:amount // 2 * 2:2], mixed[1:amount // 2 * 2:2]
    room = jnp.minimum(sizes[giver] - 1, most - sizes[sink]) // 2
    room = jnp.where((giver == ranking[0]) | (sink == ranking[0]) | (sizes[sink] == 0), 0, jnp.maximum(room, 0))
    passed = jax.random.randint(jax.random.fold_in(own, 4), (amount // 2,), 0, 1 << 20) % (room + 1)
    sizes = sizes.at[giver].add(-passed).at[sink].add(passed)
    members = jnp.searchsorted(jnp.cumsum(sizes), jnp.arange(rows * top), side="right").astype(jnp.int32)
    table = members.reshape(top, rows).T
    table = table[jax.random.permutation(jax.random.fold_in(own, 1), rows)]
    rotation = jax.random.randint(jax.random.fold_in(own, 2), (rows, 1), 0, top)
    return jnp.take_along_axis(table, (jnp.arange(top)[None, :] + rotation) % top, axis=1)


def load_shares(number_of, total, limit, lean, full):
    weights = [(1 << 20) // math.isqrt(grade ** lean) + 1 for grade in range(1, number_of + 1)]
    largest = limit if full else min(limit, max(-(-total // number_of), total * weights[0] // sum(weights)))
    least = 1 if total - largest >= number_of - 1 else 0
    given, rest = [largest] + [least] * (number_of - 1), total - largest - least * (number_of - 1)
    while rest > 0:
        free = [i for i in range(1, number_of) if given[i] < largest] or [i for i in range(1, number_of) if given[i] < limit]
        pool, left = sum([weights[i] for i in free]), rest
        for i in free:
            more = min(limit - given[i], max(1, left * weights[i] // pool), rest)
            given[i] = given[i] + more
            rest = rest - more
    return np.array(given)


def normal_values(stream_key, shape, deviation, most, pieces=(), held_as=jnp.bfloat16):
    gain = block_scale(stream_key, shape, pieces, -0.22, 0.18) if pieces else 1.0
    entries = jax.random.normal(stream_key, shape, jnp.float32) * deviation * gain
    return jnp.minimum(jnp.maximum(entries, -most), most).astype(held_as)


def setup_inputs(seed: int = 0) -> dict:
    key_list = jax.random.split(jax.random.key(seed), 12)
    e_field = normal_values(key_list[0], (3, NX, NY, NZ), 1.0, 6.0, ((1, 16), (2, 8), (3, 2)), jnp.float32)
    h_field = normal_values(key_list[1], (3, NX, NY, NZ), 1.0, 6.0, ((1, 16), (2, 8), (3, 2)), jnp.float32)
    permittivity = jnp.clip(jnp.exp(math.log(4.0) - 1.3862944 * jax.random.uniform(key_list[2], (NX, NY, NZ), jnp.float32) ** block_scale(key_list[2], (NX, NY, NZ), ((0, 16), (1, 8), (2, 2)), -0.2, 0.2)), 1.0, 4.0)
    wall_mask = plant((jax.random.randint(key_list[3], (NX, NY, NZ), 0, 4) < 1).astype(jnp.int32), jax.random.fold_in(key_list[3], 1), 0, 1)
    poles = normal_values(key_list[4], (POLES, 3, NX, NY, NZ), 0.3, 4.0, ((2, 16), (3, 8), (4, 2)), jnp.float32)
    pole_decay = jnp.clip(jnp.exp(jax.random.uniform(key_list[5], (POLES,), jnp.float32, math.log(0.2), math.log(0.95))), 0.2, 0.95)
    pole_gain = jnp.clip(jax.random.uniform(key_list[6], (POLES,), jnp.float32, 0.05, 0.3), 0.05, 0.3)
    face_cells = plant(jax.random.randint(key_list[7], (FACES,), 0, CX * CY * CZ), jax.random.fold_in(key_list[7], 1), 0, (CX * CY * CZ) - 1).astype(jnp.int32)
    owners_keys = jax.random.split(jax.random.fold_in(key_list[8], 1), FACES // K_DEV)
    owners_turns = jax.random.permutation(jax.random.fold_in(key_list[8], 3), FACES // K_DEV)
    owners = jax.vmap(lambda own, number: shared_out(jax.random.fold_in(key_list[8], 2), own, number, K_DEV, N_GX, 1, CAP, 2))(owners_keys, owners_turns).reshape((FACES, 1))
    history = normal_values(key_list[9], (STEPS - 1, 4, FACES), 1.0, 6.0, ((2, 256),))
    steering = normal_values(key_list[10], (4, ROWS, DIRS), (2 * ROWS) ** -0.5, 0.03125, ((1, 128), (2, 2)))
    return {"e_field": e_field, "h_field": h_field, "permittivity": permittivity, "wall_mask": wall_mask, "poles": poles, "pole_decay": pole_decay, "pole_gain": pole_gain, "face_cells": face_cells, "owners": owners, "history": history, "steering": steering}


def forward(field, axis):
    widths = [(0, 0), (0, 0), (0, 0)]
    widths[axis] = (0, 1)
    return lax.slice_in_dim(jnp.pad(field, widths), 1, field.shape[axis] + 1, axis=axis)

def backward(field, axis):
    widths = [(0, 0), (0, 0), (0, 0)]
    widths[axis] = (1, 0)
    return lax.slice_in_dim(jnp.pad(field, widths), 0, field.shape[axis], axis=axis)

def spectral_table(freqs, steps):
    times = jnp.arange(steps, dtype=jnp.float32)
    levels = jnp.arange(freqs, dtype=jnp.float32) + 0.5
    phase = math.pi / (2.0 * freqs) * levels[:, None] * times[None, :]
    scale = 1.0 / math.sqrt(steps)
    return jnp.stack([jnp.cos(phase) * scale, -jnp.sin(phase) * scale])

def bucket_rank(owner, groups):
    onehot = (owner[..., None] == jnp.arange(groups, dtype=jnp.int32)).astype(jnp.int32)
    return lax.optimization_barrier(jnp.sum((jnp.cumsum(onehot, axis=-2) - onehot) * onehot, axis=-1))

def reference(e_field, h_field, permittivity, wall_mask, poles, pole_decay, pole_gain, face_cells, owners, history, steering):
    elec_x, elec_y, elec_z = (e_field[0], e_field[1], e_field[2])
    mag_x = h_field[0] - 0.5 * (forward(elec_z, 1) - elec_z - (forward(elec_y, 2) - elec_y))
    mag_y = h_field[1] - 0.5 * (forward(elec_x, 2) - elec_x - (forward(elec_z, 0) - elec_z))
    mag_z = h_field[2] - 0.5 * (forward(elec_y, 0) - elec_y - (forward(elec_x, 1) - elec_x))
    drive = jnp.stack([mag_z - backward(mag_z, 1) - (mag_y - backward(mag_y, 2)), mag_x - backward(mag_x, 2) - (mag_z - backward(mag_z, 0)), mag_y - backward(mag_y, 0) - (mag_x - backward(mag_x, 1))])
    h_next = jnp.stack([mag_x, mag_y, mag_z])
    poles_next = pole_decay[:, None, None, None, None] * poles + pole_gain[:, None, None, None, None] * drive[None]
    e_next = jnp.where(wall_mask[None] == 1, lax.optimization_barrier(jnp.sum(poles_next, axis=0)), e_field + (0.5 / permittivity)[None] * drive)
    devices = N_GX * N_GY * N_GZ
    span = CX * CY * CZ

    def blocks(field):
        shaped = field.reshape(N_GX, CX, N_GY, CY, N_GZ, CZ).transpose(0, 2, 4, 1, 3, 5)
        return shaped.reshape(devices, span)
    cells = face_cells.reshape(devices, K_DEV).astype(jnp.int32)
    picked = [blocks(e_next[0]), blocks(e_next[1]), blocks(h_next[0]), blocks(h_next[1])]
    fresh = jnp.stack([jnp.take_along_axis(block, cells, axis=1).reshape(-1) for block in picked]).astype(jnp.bfloat16)
    series = jnp.concatenate([history, fresh[None]], axis=0)
    owner = owners[:, 0].reshape(devices, K_DEV).astype(jnp.int32)
    rank = bucket_rank(owner, N_GX)
    device_ids = jnp.arange(devices, dtype=jnp.int32)
    source_x = device_ids // (N_GY * N_GZ)
    source_y = device_ids // N_GZ % N_GY
    source_z = device_ids % N_GZ
    row = (owner * N_GY + source_y[:, None]) * TILE + source_z[:, None] * (N_GX * CAP) + source_x[:, None] * CAP + rank
    row = row.reshape(-1).astype(jnp.int32)
    projected = jnp.zeros((STEPS, DIRS), jnp.float32)
    for comp in range(4):
        weights = jnp.take(steering[comp], row, axis=0)
        projected = projected + jnp.dot(series[:, comp, :], weights, preferred_element_type=jnp.float32)
    table = spectral_table(FREQS, STEPS)
    far_field = jnp.einsum('sft,td->sfd', table, projected, precision=lax.Precision.HIGHEST)
    return (e_next, h_next, poles_next, far_field)
```

```python
import math

import jax
import jax.numpy as jnp
import numpy as np
from jax import lax
from jax.experimental import pallas as pl
from jax.experimental.pallas import tpu as pltpu
from jax.sharding import PartitionSpec as P

FREQS = 256
F32 = jnp.float32
BF16 = jnp.bfloat16
VM = pl.BlockSpec(memory_space=pltpu.VMEM)
SM = pl.BlockSpec(memory_space=pltpu.SMEM)


def call(body, out_shape, in_specs, scratch=(), flops=0, data=0):
    many = isinstance(out_shape, (list, tuple))
    return pl.pallas_call(
        body,
        out_shape=out_shape,
        in_specs=in_specs,
        out_specs=[VM] * len(out_shape) if many else VM,
        scratch_shapes=list(scratch),
        compiler_params=pltpu.CompilerParams(vmem_limit_bytes=32 << 20),
        cost_estimate=pl.CostEstimate(flops=flops, bytes_accessed=data, transcendentals=0),
    )


def struct(*shape, dtype=F32):
    return jax.ShapeDtypeStruct(shape, dtype)


def lanes(*shape):
    return lax.broadcasted_iota(jnp.int32, shape, len(shape) - 1)


def rows(*shape):
    return lax.broadcasted_iota(jnp.int32, shape, len(shape) - 2)


def dot_t(a, b):
    return lax.dot_general(a, b, (((0,), (0,)), ((), ())), preferred_element_type=F32)


def face_body(e_ref, fx_ref, fy_ref, fz_ref):
    nx = e_ref.shape[1]
    fx_ref[0] = e_ref[1, 0]
    fx_ref[1] = e_ref[2, 0]
    lane = lanes(16, 128)
    for part, comp in enumerate((0, 2)):
        for i in range(nx):
            fy_ref[part, i : i + 1, :] = e_ref[comp, i, 0:1, :]
    for part, comp in enumerate((0, 1)):
        acc = jnp.zeros((16, 128), F32)
        for i in range(nx):
            moved = e_ref[comp, i] if i == 0 else pltpu.roll(e_ref[comp, i], i, 1)
            acc = jnp.where(lane == i, moved, acc)
        fz_ref[part] = acc


def mag_body(keep, e_ref, h_ref, hx_ref, hy_ref, hz_ref, out_ref, gx_ref, gy_ref, gz_ref):
    nx = e_ref.shape[1]
    lane = lanes(16, 128)
    row = rows(16, 128)
    up_x = [hx_ref[part] * keep[0] for part in range(2)]
    up_y = [hy_ref[part] * keep[1] for part in range(2)]
    up_z = [hz_ref[part] * keep[2] for part in range(2)]
    face_z = [jnp.zeros((16, 128), F32), jnp.zeros((16, 128), F32)]
    for i in range(nx):
        ex, ey, ez = e_ref[0, i], e_ref[1, i], e_ref[2, i]
        ey_x = e_ref[1, i + 1] if i + 1 < nx else up_x[0]
        ez_x = e_ref[2, i + 1] if i + 1 < nx else up_x[1]
        ex_y = jnp.where(row == 15, up_y[0][i : i + 1], pltpu.roll(ex, 15, 0))
        ez_y = jnp.where(row == 15, up_y[1][i : i + 1], pltpu.roll(ez, 15, 0))
        ex_z = jnp.where(lane == 127, pltpu.roll(up_z[0], 127 - i, 1), pltpu.roll(ex, 127, 1))
        ey_z = jnp.where(lane == 127, pltpu.roll(up_z[1], 127 - i, 1), pltpu.roll(ey, 127, 1))
        hx = h_ref[0, i] - 0.5 * ((ez_y - ez) - (ey_z - ey))
        hy = h_ref[1, i] - 0.5 * ((ex_z - ex) - (ez_x - ez))
        hz = h_ref[2, i] - 0.5 * ((ey_x - ey) - (ex_y - ex))
        out_ref[0, i] = hx
        out_ref[1, i] = hy
        out_ref[2, i] = hz
        if i == nx - 1:
            gx_ref[0] = hy
            gx_ref[1] = hz
        gy_ref[0, i : i + 1, :] = hx[15:16]
        gy_ref[1, i : i + 1, :] = hz[15:16]
        for part, value in enumerate((hx, hy)):
            face_z[part] = jnp.where(lane == i, pltpu.roll(value, (i + 1) % 128, 1), face_z[part])
    gz_ref[0] = face_z[0]
    gz_ref[1] = face_z[1]


def decay_body(decay, poles_ref, out_ref):
    for comp in range(3):
        for i in range(poles_ref.shape[2]):
            acc = decay[0] * poles_ref[0, comp, i]
            for p in range(1, poles_ref.shape[0]):
                acc = acc + decay[p] * poles_ref[p, comp, i]
            out_ref[comp, i] = acc


def elec_body(
    keep, gain, e_ref, h_ref, hx_ref, hy_ref, hz_ref, eps_ref, wall_ref, kept_ref, prep_ref,
    e_out, drive_out, pack_out, cells,
):
    nx = e_ref.shape[1]
    lane = lanes(16, 128)
    row = rows(16, 128)
    dn_x = [hx_ref[part] * keep[3] for part in range(2)]
    dn_y = [hy_ref[part] * keep[4] for part in range(2)]
    dn_z = [hz_ref[part] * keep[5] for part in range(2)]
    total = gain[0]
    for p in range(1, gain.shape[0]):
        total = total + gain[p]
    for i in range(nx):
        hx, hy, hz = h_ref[0, i], h_ref[1, i], h_ref[2, i]
        hy_x = h_ref[1, i - 1] if i else dn_x[0]
        hz_x = h_ref[2, i - 1] if i else dn_x[1]
        hx_y = jnp.where(row == 0, dn_y[0][i : i + 1], pltpu.roll(hx, 1, 0))
        hz_y = jnp.where(row == 0, dn_y[1][i : i + 1], pltpu.roll(hz, 1, 0))
        low = [v if i == 0 else pltpu.roll(v, 128 - i, 1) for v in dn_z]
        hx_z = jnp.where(lane == 0, low[0], pltpu.roll(hx, 1, 1))
        hy_z = jnp.where(lane == 0, low[1], pltpu.roll(hy, 1, 1))
        drive = [
            (hz - hz_y) - (hy - hy_z),
            (hx - hx_z) - (hz - hz_x),
            (hy - hy_x) - (hx - hx_y),
        ]
        half = 0.5 / eps_ref[i]
        wall = wall_ref[i] == 1
        for comp in range(3):
            field = jnp.where(
                wall, kept_ref[comp, i] + total * drive[comp], e_ref[comp, i] + half * drive[comp]
            )
            e_out[comp, i] = field
            drive_out[comp, i] = drive[comp]
            if comp < 2:
                cells[comp, i * 16 : (i + 1) * 16, :] = field.astype(BF16)
        cells[2, i * 16 : (i + 1) * 16, :] = hx.astype(BF16)
        cells[3, i * 16 : (i + 1) * 16, :] = hy.astype(BF16)
    pick = prep_ref[2].astype(BF16)
    at = prep_ref[3]
    lane = lanes(32, 128)
    packed = jnp.zeros((128, 128), F32)
    for half in range(2):
        wide = jnp.zeros((32, 128), F32)
        for e in range(2):
            found = jnp.dot(pick, cells[2 * half + e], preferred_element_type=F32)
            value = jnp.sum(found * at, axis=1, keepdims=True)
            wide = jnp.where(lane == 64 * e + 63, value, wide)
        packed = packed + dot_t(prep_ref[half].astype(BF16), wide.astype(BF16))
    pack_out[0] = packed
    pack_out[1] = packed


def poles_body(decay, gain, poles_ref, drive_ref, out_ref):
    for comp in range(3):
        for i in range(poles_ref.shape[2]):
            drive = drive_ref[comp, i]
            for p in range(poles_ref.shape[0]):
                out_ref[p, comp, i] = decay[p] * poles_ref[p, comp, i] + gain[p] * drive


def pack_body(owner_ref, cell_ref, hist_ref, prep_out, pack_out):
    lane = lanes(32, 128)
    owner = owner_ref[...]
    onehot = jnp.where(lane == owner, 1.0, 0.0)
    earlier = jnp.where(lanes(32, 32) < rows(32, 32), 1.0, 0.0).astype(BF16)
    count = jnp.dot(earlier, onehot.astype(BF16), preferred_element_type=F32)
    rank = jnp.sum(count * onehot, axis=1, keepdims=True).astype(jnp.int32)
    slot = owner * 8 + rank
    cell = cell_ref[...]
    prep_out[2] = jnp.where(lane == (cell >> 7), 1.0, 0.0)
    prep_out[3] = jnp.where(lane == (cell & 127), 1.0, 0.0)
    packed = jnp.zeros((128, 128), F32)
    for half in range(2):
        select = jnp.where(lane == slot + 4 * half, 1.0, 0.0)
        prep_out[half] = select
        packed = packed + lax.dot_general(
            select.T.astype(BF16),
            hist_ref[half * 128 : (half + 1) * 128, :],
            (((1,), (1,)), ((), ())),
            preferred_element_type=F32,
        )
    pack_out[0] = packed
    pack_out[1] = packed


def tile_rows(got_ref, first):
    got = got_ref[...].astype(BF16)
    row, slot = rows(256, 128), lanes(256, 128)
    parts = []
    for half in range(2):
        place = jnp.where(row == (slot >> 2) * 8 + 4 * half + (slot & 3), 1.0, 0.0).astype(BF16)
        moved = dot_t(got, place).astype(BF16)
        parts += [moved[first:64], moved[64 + first : 128]]
    return jnp.concatenate(parts, axis=1)


def project_body(got_ref, steer_ref, out_ref):
    series = tile_rows(got_ref, 0)
    for n in range(8):
        part = jnp.dot(series, steer_ref[:, n * 256 : (n + 1) * 256], preferred_element_type=F32)
        out_ref[2 * n] = part[:, :128]
        out_ref[2 * n + 1] = part[:, 128:]


def spectrum_body(got_ref, steer_ref, sums_ref, table_ref, out_ref, last):
    series = tile_rows(got_ref, 48)
    for n in range(8):
        part = jnp.dot(series, steer_ref[:, n * 256 : (n + 1) * 256], preferred_element_type=F32)
        last[2 * n : 2 * n + 1, :] = part[15:16, :128]
        last[2 * n + 1 : 2 * n + 2, :] = part[15:16, 128:]
    projected = sums_ref[0]
    for a in range(1, sums_ref.shape[0]):
        projected = projected + sums_ref[a]
    for b in range(8):
        out_ref[b, 0:64, :] = jnp.dot(
            table_ref[b], projected, precision=lax.Precision.HIGHEST, preferred_element_type=F32
        )
        out_ref[b, 64:80, :] = last[...]


def regroup_body(got_ref, out_ref):
    total = got_ref[0]
    for b in range(1, got_ref.shape[0]):
        total = total + got_ref[b]
    for a in range(16):
        out_ref[a, 0:4, :] = total[4 * a : 4 * a + 4]
        out_ref[a, 8:24, :] = total[64:80]


def finish_body(weight, got_ref, out_ref):
    last = got_ref[0, 8:24, :]
    for a in range(1, 16):
        last = last + got_ref[a, 8:24, :]
    for a in range(16):
        for s in range(2):
            for f in range(2):
                out_ref[s, f : f + 1, a * 128 : (a + 1) * 128] = (
                    got_ref[a, 2 * s + f : 2 * s + f + 1, :] + weight[s, f] * last[a : a + 1]
                )


def spectral_table(steps):
    times = np.arange(steps, dtype=np.float64)
    levels = np.arange(FREQS, dtype=np.float64) + 0.5
    phase = math.pi / (2.0 * FREQS) * levels[:, None] * times[None, :]
    table = np.stack([np.cos(phase), -np.sin(phase)]) / math.sqrt(steps)
    return table.astype(np.float32)


def shift(value, axis, step):
    count = lax.axis_size(axis)
    return lax.ppermute(value, axis, [(i, (i + step) % count) for i in range(count)])


def per_device(
    e_field, h_field, permittivity, wall_mask, poles, pole_decay, pole_gain, face_cells, owners,
    history, steering,
):
    nx, ny, nz = e_field.shape[1:]
    steps = history.shape[0] + 1
    axes = ("gx", "gy", "gz")
    places = [lax.axis_index(axis) for axis in axes]
    keep = jnp.stack(
        [(at < lax.axis_size(axis) - 1) for at, axis in zip(places, axes)]
        + [at > 0 for at in places]
    ).astype(F32)
    block = struct(3, nx, ny, nz)
    faces = [struct(2, ny, nz), struct(2, nx, nz), struct(2, ny, 128)]

    near = call(face_body, faces, [VM], data=200000)(e_field)
    up = [shift(face, axis, -1) for face, axis in zip(near, axes)]

    past = jnp.transpose(history, (1, 0, 2))
    past = jnp.pad(past, ((0, 0), (0, 1), (0, 0))).reshape(4 * steps, -1)
    prep, leaving = call(pack_body, [struct(4, 32, 128), struct(2, 128, 128)], [VM] * 3, data=200000)(
        owners, face_cells.reshape(-1, 1), past
    )

    def to_tiles(packed):
        moved = lax.all_to_all(packed.reshape(32, 8, 128), ("gz", "gx"), 0, 0, tiled=True)
        return moved.reshape(256, 128)

    arrived = to_tiles(leaving)

    h_next, *far = call(mag_body, [block, *faces], [SM] + [VM] * 5, data=600000)(
        keep, e_field, h_field, *up
    )
    down = [shift(face, axis, 1) for face, axis in zip(far, axes)]
    kept = call(decay_body, block, [SM, VM], data=1800000)(pole_decay, poles)

    weights = steering.reshape(-1, steering.shape[2])
    part = call(project_body, struct(16, 64, 128), [VM] * 2, flops=1 << 27, data=2600000)(
        arrived, weights
    )
    sums = lax.all_to_all(part, "gx", 0, 0, tiled=True)

    e_next, drive, fresh = call(
        elec_body,
        [block, block, struct(2, 128, 128)],
        [SM] * 2 + [VM] * 9,
        scratch=[pltpu.VMEM((4, 128, 128), BF16)],
        data=1200000,
    )(keep, pole_gain, e_field, h_next, *down, permittivity, wall_mask, kept, prep)
    latest = to_tiles(fresh)
    poles_next = call(poles_body, struct(*poles.shape), [SM] * 2 + [VM] * 2, data=3400000)(
        pole_decay, pole_gain, poles, drive
    )

    table = spectral_table(steps)
    ordered = table.reshape(2, 16, 8, 2, steps).transpose(2, 1, 0, 3, 4).reshape(8, 64, steps)
    spectra = call(
        spectrum_body,
        struct(8, 80, 128),
        [VM] * 4,
        scratch=[pltpu.VMEM((16, 128), F32)],
        flops=1 << 27,
        data=2600000,
    )(latest, weights, sums, jnp.asarray(ordered))
    spectra = lax.all_to_all(spectra, "gy", 0, 0, tiled=True)
    blocks = call(regroup_body, struct(16, 24, 128), [VM], data=500000)(spectra)
    blocks = lax.all_to_all(blocks, "gx", 0, 0, tiled=True)
    mine = places[0] * 8 + places[1]
    weight = lax.dynamic_slice(jnp.asarray(table[:, :, -1]), (0, 2 * mine), (2, 2))
    far_field = call(finish_body, struct(2, 2, 2048), [SM, VM], data=200000)(weight, blocks)
    return (e_next, h_next, poles_next, far_field)


def solution(mesh):
    return jax.shard_map(
        per_device,
        mesh=mesh,
        in_specs=(
            P(None, "gx", "gy", "gz"),
            P(None, "gx", "gy", "gz"),
            P("gx", "gy", "gz"),
            P("gx", "gy", "gz"),
            P(None, None, "gx", "gy", "gz"),
            P(),
            P(),
            P(("gx", "gy", "gz")),
            P(("gx", "gy", "gz"), None),
            P(None, None, ("gx", "gy", "gz")),
            P(None, ("gx", "gy"), "gz"),
        ),
        out_specs=(
            P(None, "gx", "gy", "gz"),
            P(None, "gx", "gy", "gz"),
            P(None, None, "gx", "gy", "gz"),
            P(None, ("gx", "gy"), "gz"),
        ),
        check_vma=False,
    )
```

```python
import math

import jax
import jax.numpy as jnp
import numpy as np
from jax import lax
from jax.experimental import pallas as pl
from jax.experimental.pallas import tpu as pltpu
from jax.sharding import PartitionSpec as P

FREQS = 256
F32 = jnp.float32
BF16 = jnp.bfloat16
VM = pl.BlockSpec(memory_space=pltpu.VMEM)
SM = pl.BlockSpec(memory_space=pltpu.SMEM)
HB = pl.BlockSpec(memory_space=pltpu.HBM)


def call(body, out_shape, in_specs, scratch=(), flops=0, data=0):
    many = isinstance(out_shape, (list, tuple))
    return pl.pallas_call(
        body,
        out_shape=out_shape,
        in_specs=in_specs,
        out_specs=[VM] * len(out_shape) if many else VM,
        scratch_shapes=list(scratch),
        compiler_params=pltpu.CompilerParams(vmem_limit_bytes=32 << 20),
        cost_estimate=pl.CostEstimate(flops=flops, bytes_accessed=data, transcendentals=0),
    )


def far_off(value):
    return pltpu.with_memory_space_constraint(value, pltpu.HBM)


def struct(*shape, dtype=F32):
    return jax.ShapeDtypeStruct(shape, dtype)


def lanes(*shape):
    return lax.broadcasted_iota(jnp.int32, shape, len(shape) - 1)


def rows(*shape):
    return lax.broadcasted_iota(jnp.int32, shape, len(shape) - 2)


def dot_t(a, b):
    return lax.dot_general(a, b, (((0,), (0,)), ((), ())), preferred_element_type=F32)


def fetch(pairs, sems):
    copies = [pltpu.make_async_copy(*pair, sems.at[n]) for n, pair in enumerate(pairs)]
    for copy in copies:
        copy.start()
    return copies


def face_body(e_far, h_far, fx_ref, fy_ref, fz_ref, e_ref, h_ref, sems):
    bring = fetch([(e_far, e_ref), (h_far, h_ref)], sems)
    bring[0].wait()
    nx = e_ref.shape[1]
    fx_ref[0] = e_ref[1, 0]
    fx_ref[1] = e_ref[2, 0]
    lane = lanes(16, 128)
    for part, comp in enumerate((0, 2)):
        for i in range(nx):
            fy_ref[part, i : i + 1, :] = e_ref[comp, i, 0:1, :]
    for part, comp in enumerate((0, 1)):
        acc = jnp.zeros((16, 128), F32)
        for i in range(nx):
            moved = e_ref[comp, i] if i == 0 else pltpu.roll(e_ref[comp, i], i, 1)
            acc = jnp.where(lane == i, moved, acc)
        fz_ref[part] = acc
    bring[1].wait()


def inner_body(e_ref, h_ref, *refs):
    count = (len(refs) - 2) // 2
    out_ref, sems = refs[count], refs[-1]
    bring = fetch(list(zip(refs[:count], refs[count + 1 : -1])), sems)
    nx = e_ref.shape[1]
    lane = lanes(16, 128)
    row = rows(16, 128)
    zero = jnp.zeros((16, 128), F32)
    for i in range(nx):
        ex, ey, ez = e_ref[0, i], e_ref[1, i], e_ref[2, i]
        ey_x = e_ref[1, i + 1] if i + 1 < nx else zero
        ez_x = e_ref[2, i + 1] if i + 1 < nx else zero
        ex_y = jnp.where(row == 15, 0.0, pltpu.roll(ex, 15, 0))
        ez_y = jnp.where(row == 15, 0.0, pltpu.roll(ez, 15, 0))
        ex_z = jnp.where(lane == 127, 0.0, pltpu.roll(ex, 127, 1))
        ey_z = jnp.where(lane == 127, 0.0, pltpu.roll(ey, 127, 1))
        out_ref[0, i] = h_ref[0, i] - 0.5 * ((ez_y - ez) - (ey_z - ey))
        out_ref[1, i] = h_ref[1, i] - 0.5 * ((ex_z - ex) - (ez_x - ez))
        out_ref[2, i] = h_ref[2, i] - 0.5 * ((ey_x - ey) - (ex_y - ex))
    for copy in bring:
        copy.wait()


def mag_body(keep, part_ref, ux_ref, uy_ref, uz_ref, out_ref, gx_ref, gy_ref, gz_ref):
    nx = part_ref.shape[1]
    lane = lanes(16, 128)
    row = rows(16, 128)
    up_x = [ux_ref[part] * (0.5 * keep[0]) for part in range(2)]
    up_y = [uy_ref[part] * (0.5 * keep[1]) for part in range(2)]
    up_z = [uz_ref[part] * (0.5 * keep[2]) for part in range(2)]
    face_z = [jnp.zeros((16, 128), F32), jnp.zeros((16, 128), F32)]
    for i in range(nx):
        ex_z, ey_z = [jnp.where(lane == 127, pltpu.roll(v, 127 - i, 1), 0.0) for v in up_z]
        ex_y, ez_y = [jnp.where(row == 15, v[i : i + 1], 0.0) for v in up_y]
        hx = part_ref[0, i] + (ey_z - ez_y)
        hy = part_ref[1, i] - ex_z
        hz = part_ref[2, i] + ex_y
        if i == nx - 1:
            hy = hy + up_x[1]
            hz = hz - up_x[0]
            gx_ref[0] = hy
            gx_ref[1] = hz
        out_ref[0, i] = hx
        out_ref[1, i] = hy
        out_ref[2, i] = hz
        gy_ref[0, i : i + 1, :] = hx[15:16]
        gy_ref[1, i : i + 1, :] = hz[15:16]
        for part, value in enumerate((hx, hy)):
            face_z[part] = jnp.where(lane == i, pltpu.roll(value, i + 1, 1), face_z[part])
    gz_ref[0] = face_z[0]
    gz_ref[1] = face_z[1]


def wall_body(decay_ref, gain_ref, poles_ref, e_ref, eps_ref, wall_ref, base_out, slope_out):
    decay = [decay_ref[0:1, p : p + 1] for p in range(poles_ref.shape[0])]
    total = jnp.sum(gain_ref[...], axis=1, keepdims=True)
    for i in range(poles_ref.shape[2]):
        wall = wall_ref[i] == 1
        slope_out[i] = jnp.where(wall, total, 0.5 / eps_ref[i])
        for comp in range(3):
            acc = decay[0] * poles_ref[0, comp, i]
            for p in range(1, poles_ref.shape[0]):
                acc = acc + decay[p] * poles_ref[p, comp, i]
            base_out[comp, i] = jnp.where(wall, acc, e_ref[comp, i])


def elec_body(
    keep, h_ref, dx_ref, dy_ref, dz_ref, base_ref, slope_ref, select_ref, cell_ref, past_ref,
    drive_out, pack_out, cells,
):
    nx = h_ref.shape[1]
    lane = lanes(16, 128)
    row = rows(16, 128)
    dn_x = [dx_ref[part] * keep[3] for part in range(2)]
    dn_y = [dy_ref[part] * keep[4] for part in range(2)]
    dn_z = [dz_ref[part] * keep[5] for part in range(2)]
    for i in range(nx):
        hx, hy, hz = h_ref[0, i], h_ref[1, i], h_ref[2, i]
        hy_x = h_ref[1, i - 1] if i else dn_x[0]
        hz_x = h_ref[2, i - 1] if i else dn_x[1]
        hx_y = jnp.where(row == 0, dn_y[0][i : i + 1], pltpu.roll(hx, 1, 0))
        hz_y = jnp.where(row == 0, dn_y[1][i : i + 1], pltpu.roll(hz, 1, 0))
        low = [v if i == 0 else pltpu.roll(v, 128 - i, 1) for v in dn_z]
        hx_z = jnp.where(lane == 0, low[0], pltpu.roll(hx, 1, 1))
        hy_z = jnp.where(lane == 0, low[1], pltpu.roll(hy, 1, 1))
        drive = [
            (hz - hz_y) - (hy - hy_z),
            (hx - hx_z) - (hz - hz_x),
            (hy - hy_x) - (hx - hx_y),
        ]
        for comp in range(3):
            drive_out[comp, i] = drive[comp]
        span = pl.ds(i * 16, 16)
        for comp in range(2):
            field = base_ref[comp, i] + slope_ref[i] * drive[comp]
            cells[comp, span, :] = field.astype(BF16)
        cells[2, span, :] = hx.astype(BF16)
        cells[3, span, :] = hy.astype(BF16)
    pick = cell_ref[0].astype(BF16)
    at = cell_ref[1]
    lane = lanes(32, 128)
    packed = past_ref[...]
    for half in range(2):
        wide = jnp.zeros((32, 128), F32)
        for e in range(2):
            found = jnp.dot(pick, cells[2 * half + e], preferred_element_type=F32)
            value = jnp.sum(found * at, axis=1, keepdims=True)
            wide = jnp.where(lane == 64 * e + 63, value, wide)
        packed = packed + jnp.dot(
            select_ref[half].astype(BF16), wide.astype(BF16), preferred_element_type=F32
        )
    pack_out[0] = packed
    pack_out[1] = packed


def state_body(
    decay_ref, gain_ref, poles_ref, drive_ref, base_ref, slope_ref, h_ref, p_out, e_out, h_out
):
    decay = [decay_ref[0:1, p : p + 1] for p in range(poles_ref.shape[0])]
    gain = [gain_ref[0:1, p : p + 1] for p in range(poles_ref.shape[0])]
    for i in range(poles_ref.shape[2]):
        for comp in range(3):
            drive = drive_ref[comp, i]
            e_out[comp, i] = base_ref[comp, i] + slope_ref[i] * drive
            h_out[comp, i] = h_ref[comp, i]
            for p in range(poles_ref.shape[0]):
                p_out[p, comp, i] = decay[p] * poles_ref[p, comp, i] + gain[p] * drive


def pack_body(owner_ref, cell_ref, hist_ref, select_out, cell_out, pack_out):
    owner = owner_ref[...]
    onehot = jnp.where(rows(16, 32) == owner, 1.0, 0.0)
    earlier = jnp.where(rows(32, 32) < lanes(32, 32), 1.0, 0.0).astype(BF16)
    count = jnp.dot(onehot.astype(BF16), earlier, preferred_element_type=F32)
    rank = jnp.sum(count * onehot, axis=0, keepdims=True).astype(jnp.int32)
    slot = owner * 8 + rank
    cell = cell_ref[...]
    row = rows(128, 32)
    cell_out[0] = jnp.where(row == (cell >> 7), 1.0, 0.0).T
    cell_out[1] = jnp.where(row == (cell & 127), 1.0, 0.0).T
    packed = jnp.zeros((128, 128), F32)
    for half in range(2):
        select = jnp.where(row == slot + 4 * half, 1.0, 0.0)
        select_out[half] = select
        gap = jnp.zeros((32, 1), F32)
        past = [hist_ref[2 * half + e].astype(F32) for e in range(2)]
        past = jnp.concatenate([past[0], gap, past[1], gap], axis=1)
        packed = packed + jnp.dot(
            select.astype(BF16), past.astype(BF16), preferred_element_type=F32
        )
    pack_out[...] = packed


def project_body(core, got_ref, steer_ref, series_out, out_ref):
    got = got_ref[...].astype(BF16)
    row, slot = rows(256, 128), lanes(256, 128)
    parts = []
    for half in range(2):
        place = jnp.where(row == (slot >> 2) * 8 + 4 * half + (slot & 3), 1.0, 0.0).astype(BF16)
        moved = dot_t(got, place).astype(BF16)
        parts += [moved[:64], moved[64:]]
    series = jnp.concatenate(parts, axis=1)
    series_out[...] = series
    project_half(1 - core[0], series, steer_ref, out_ref, None)


def project_half(half, series, steer_ref, out_ref, add_ref):
    for n in range(4):
        first = pl.multiple_of(half * 1024 + n * 256, 256)
        part = jnp.dot(series, steer_ref[:, pl.ds(first, 256)], preferred_element_type=F32)
        for m in range(2):
            piece = part[:, m * 128 : (m + 1) * 128]
            out_ref[2 * n + m] = piece if add_ref is None else piece + add_ref[2 * n + m]


def project_own_body(core, series_ref, steer_ref, add_ref, out_ref):
    project_half(core[0], series_ref[...], steer_ref, out_ref, add_ref)


def sum_body(got_ref, out_ref):
    total = got_ref[0]
    for a in range(1, got_ref.shape[0]):
        total = total + got_ref[a]
    out_ref[...] = total


def spectrum_body(core, mine_ref, other_ref, table_ref, out_ref):
    mine, other = mine_ref[...], other_ref[...]
    first = core[0] == 0
    both = jnp.concatenate([jnp.where(first, mine, other), jnp.where(first, other, mine)], axis=0)
    high = both.astype(BF16)
    low = (both - high.astype(F32)).astype(BF16)
    out_ref[...] = jnp.dot(
        table_ref[core[0]], jnp.concatenate([high, low, high], axis=0), preferred_element_type=F32
    )


def finish_body(got_ref, out_ref):
    for g in range(8):
        total = got_ref[8 * g]
        for b in range(1, 8):
            total = total + got_ref[8 * g + b]
        for half in range(2):
            first = (8 * half + g) * 128
            for s in range(2):
                at = 4 * half + 2 * s
                out_ref[s, :, first : first + 128] = total[at : at + 2]


def spectral_table(steps):
    times = np.arange(steps, dtype=np.float64)
    levels = np.arange(FREQS, dtype=np.float64) + 0.5
    phase = math.pi / (2.0 * FREQS) * levels[:, None] * times[None, :]
    table = np.stack([np.cos(phase), -np.sin(phase)]) / math.sqrt(steps)
    return table.astype(np.float32)


def peer_table(steps):
    table = spectral_table(steps).reshape(2, 8, 2, 8, 2, steps).transpose(2, 1, 3, 0, 4, 5)
    wide = np.zeros((2, 8, 8, 2, 2, 2, 2, steps), np.float32)
    for half in range(2):
        wide[:, :, :, half, :, :, half, :] = table
    wide = wide.reshape(2, 512, 2 * steps)
    high = wide.astype(jnp.bfloat16)
    low = (wide - high.astype(np.float32)).astype(jnp.bfloat16)
    return jnp.asarray(np.concatenate([high, high, low], axis=2))


def shift(value, axis, step):
    count = lax.axis_size(axis)
    return lax.ppermute(value, axis, [(i, (i + step) % count) for i in range(count)])


def per_device(
    e_field, h_field, permittivity, wall_mask, poles, pole_decay, pole_gain, face_cells, owners,
    history, steering,
):
    nx, ny, nz = e_field.shape[1:]
    steps = history.shape[0] + 1
    axes = (GX, "gy", "gz")
    places = [lax.axis_index(axis) for axis in axes]
    keep = jnp.stack(
        [(at < lax.axis_size(axis) - 1) for at, axis in zip(places, axes)]
        + [at > 0 for at in places]
    ).astype(F32)
    core = lax.axis_index("core").reshape(1)
    block = struct(3, nx, ny, nz)
    faces = [struct(2, ny, nz), struct(2, nx, nz), struct(2, ny, 128)]

    *near, e_near, h_near = call(
        face_body, [*faces, block, block], [HB] * 2, [pltpu.SemaphoreType.DMA((2,))], data=400000
    )(far_off(e_field), far_off(h_field))
    up = [shift(face, axis, -1) for face, axis in zip(near, axes)]
    near, e_near, h_near = lax.optimization_barrier((near, e_near, h_near))
    later = [
        poles, permittivity, wall_mask, pole_decay.reshape(1, -1), pole_gain.reshape(1, -1),
        owners.reshape(1, -1), face_cells.reshape(1, -1), jnp.transpose(history, (1, 2, 0)),
    ]
    inner, poles, permittivity, wall_mask, decay, gain, owners, face_cells, history = call(
        inner_body,
        [block, *[struct(*value.shape, dtype=value.dtype) for value in later]],
        [VM] * 2 + [HB] * len(later),
        [pltpu.SemaphoreType.DMA((len(later),))],
        data=2600000,
    )(e_near, h_near, *[far_off(value) for value in later])

    h_mid, *far = call(mag_body, [block, *faces], [SM] + [VM] * 4, data=500000)(keep, inner, *up)
    down = [shift(face, axis, 1) for face, axis in zip(far, axes)]
    far, owners, poles = lax.optimization_barrier((far, owners, poles))
    select, cell, leaving = call(
        pack_body,
        [struct(2, 128, 32), struct(2, 32, 128), struct(128, 128)],
        [VM] * 3,
        data=200000,
    )(owners, face_cells, history)
    base, slope = call(wall_body, [block, struct(nx, ny, nz)], [VM] * 6, data=2400000)(
        decay, gain, poles, e_near, permittivity, wall_mask
    )

    drive, leaving = call(
        elec_body,
        [block, struct(2, 128, 128)],
        [SM] + [VM] * 9,
        scratch=[pltpu.VMEM((4, 128, 128), BF16)],
        data=1200000,
    )(keep, h_mid, *down, base, slope, select, cell, leaving)
    arrived = lax.all_to_all(leaving.reshape(32, 8, 128), ("gz", *GX), 0, 0, tiled=True)
    poles_next, e_next, h_next = call(
        state_body,
        [struct(*poles.shape), block, block],
        [VM] * 7,
        data=4500000,
    )(decay, gain, poles, drive, base, slope, h_mid)

    weights = steering.reshape(-1, steering.shape[2])
    series, part = call(
        project_body,
        [struct(64, 512, dtype=BF16), struct(8, 64, 128)],
        [SM] + [VM] * 2,
        flops=1 << 26,
        data=2600000,
    )(core, arrived.reshape(256, 128), weights)
    swap = [(0, 1), (1, 0)]
    part = lax.ppermute(part, "core", swap)
    series, poles_next = lax.optimization_barrier((series, poles_next))
    part = call(project_own_body, struct(8, 64, 128), [SM] + [VM] * 3, flops=1 << 26, data=2600000)(
        core, series, weights, part
    )
    part = lax.all_to_all(part, "gxc", 0, 0, tiled=True)
    mine = call(sum_body, struct(64, 128), [VM], data=300000)(part)
    other = lax.ppermute(mine, "core", swap)
    spectra = call(spectrum_body, struct(512, 128), [SM] + [VM] * 3, flops=1 << 27, data=900000)(
        core, mine, other, peer_table(steps)
    )
    spectra = lax.all_to_all(spectra.reshape(64, 8, 128), ("gxc", "gy"), 0, 0, tiled=True)
    far_field = call(finish_body, struct(2, 2, 2048), [VM], data=300000)(spectra)
    return (e_next, h_next, poles_next, far_field)


GX = ("gxc", "core")


def solution(mesh):
    shape = (mesh.shape["gx"] // 2, 2, mesh.shape["gy"], mesh.shape["gz"])
    mesh = jax.sharding.Mesh(mesh.devices.reshape(shape), ("gxc", "core", "gy", "gz"))
    return jax.shard_map(
        per_device,
        mesh=mesh,
        in_specs=(
            P(None, GX, "gy", "gz"),
            P(None, GX, "gy", "gz"),
            P(GX, "gy", "gz"),
            P(GX, "gy", "gz"),
            P(None, None, GX, "gy", "gz"),
            P(),
            P(),
            P((*GX, "gy", "gz")),
            P((*GX, "gy", "gz"), None),
            P(None, None, (*GX, "gy", "gz")),
            P(None, (*GX, "gy"), "gz"),
        ),
        out_specs=(
            P(None, GX, "gy", "gz"),
            P(None, GX, "gy", "gz"),
            P(None, None, GX, "gy", "gz"),
            P(None, (*GX, "gy"), "gz"),
        ),
        check_vma=False,
    )
```

```python
import math

import jax
import jax.numpy as jnp
import numpy as np
from jax import lax
from jax.experimental import pallas as pl
from jax.experimental.pallas import tpu as pltpu
from jax.sharding import PartitionSpec as P

FREQS = 256
F32 = jnp.float32
BF16 = jnp.bfloat16
VM = pl.BlockSpec(memory_space=pltpu.VMEM)
SM = pl.BlockSpec(memory_space=pltpu.SMEM)
HB = pl.BlockSpec(memory_space=pltpu.HBM)


def call(body, out_shape, in_specs, scratch=(), flops=0, data=0):
    many = isinstance(out_shape, (list, tuple))
    return pl.pallas_call(
        body,
        out_shape=out_shape,
        in_specs=in_specs,
        out_specs=[VM] * len(out_shape) if many else VM,
        scratch_shapes=list(scratch),
        compiler_params=pltpu.CompilerParams(vmem_limit_bytes=32 << 20),
        cost_estimate=pl.CostEstimate(flops=flops, bytes_accessed=data, transcendentals=0),
    )


def far_off(value):
    return pltpu.with_memory_space_constraint(value, pltpu.HBM)


def struct(*shape, dtype=F32):
    return jax.ShapeDtypeStruct(shape, dtype)


def lanes(*shape):
    return lax.broadcasted_iota(jnp.int32, shape, len(shape) - 1)


def rows(*shape):
    return lax.broadcasted_iota(jnp.int32, shape, len(shape) - 2)


def dot_t(a, b):
    return lax.dot_general(a, b, (((0,), (0,)), ((), ())), preferred_element_type=F32)


def fetch(pairs, sems):
    copies = [pltpu.make_async_copy(*pair, sems.at[n]) for n, pair in enumerate(pairs)]
    for copy in copies:
        copy.start()
    return copies


def face_body(e_far, h_far, fx_ref, fy_ref, fz_ref, e_ref, h_ref, sems):
    bring = fetch([(e_far, e_ref), (h_far, h_ref)], sems)
    bring[0].wait()
    nx = e_ref.shape[1]
    fx_ref[0] = e_ref[1, 0]
    fx_ref[1] = e_ref[2, 0]
    lane = lanes(16, 128)
    fy_ref[...] = jnp.zeros_like(fy_ref)
    for part, comp in enumerate((0, 2)):
        for i in range(nx):
            fy_ref[part, i : i + 1, :] = e_ref[comp, i, 0:1, :]
    for part, comp in enumerate((0, 1)):
        acc = jnp.zeros((16, 128), F32)
        for i in range(nx):
            moved = e_ref[comp, i] if i == 0 else pltpu.roll(e_ref[comp, i], i, 1)
            acc = jnp.where(lane == i, moved, acc)
        fz_ref[part, 0:16, :] = acc
        fz_ref[part, 16:24, :] = jnp.zeros((8, 128), F32)
    bring[1].wait()


def inner_body(e_ref, h_ref, *refs):
    count = (len(refs) - 2) // 2
    out_ref, sems = refs[count], refs[-1]
    bring = fetch(list(zip(refs[:count], refs[count + 1 : -1])), sems)
    nx = e_ref.shape[1]
    lane = lanes(16, 128)
    row = rows(16, 128)
    zero = jnp.zeros((16, 128), F32)
    for i in range(nx):
        ex, ey, ez = e_ref[0, i], e_ref[1, i], e_ref[2, i]
        ey_x = e_ref[1, i + 1] if i + 1 < nx else zero
        ez_x = e_ref[2, i + 1] if i + 1 < nx else zero
        ex_y = jnp.where(row == 15, 0.0, pltpu.roll(ex, 15, 0))
        ez_y = jnp.where(row == 15, 0.0, pltpu.roll(ez, 15, 0))
        ex_z = jnp.where(lane == 127, 0.0, pltpu.roll(ex, 127, 1))
        ey_z = jnp.where(lane == 127, 0.0, pltpu.roll(ey, 127, 1))
        out_ref[0, i] = h_ref[0, i] - 0.5 * ((ez_y - ez) - (ey_z - ey))
        out_ref[1, i] = h_ref[1, i] - 0.5 * ((ex_z - ex) - (ez_x - ez))
        out_ref[2, i] = h_ref[2, i] - 0.5 * ((ey_x - ey) - (ex_y - ex))
    for copy in bring:
        copy.wait()


def mag_body(keep, part_ref, ux_ref, uy_ref, uz_ref, out_ref, gx_ref, gy_ref, gz_ref):
    nx = part_ref.shape[1]
    lane = lanes(16, 128)
    row = rows(16, 128)
    up_x = [ux_ref[part] * (0.5 * keep[0]) for part in range(2)]
    up_y = [uy_ref[part] * (0.5 * keep[1]) for part in range(2)]
    up_z = [uz_ref[part, 0:16, :] * (0.5 * keep[2]) for part in range(2)]
    face_z = [jnp.zeros((16, 128), F32), jnp.zeros((16, 128), F32)]
    gy_ref[...] = jnp.zeros_like(gy_ref)
    for i in range(nx):
        ex_z, ey_z = [jnp.where(lane == 127, pltpu.roll(v, 127 - i, 1), 0.0) for v in up_z]
        ex_y, ez_y = [jnp.where(row == 15, v[i : i + 1], 0.0) for v in up_y]
        hx = part_ref[0, i] + (ey_z - ez_y)
        hy = part_ref[1, i] - ex_z
        hz = part_ref[2, i] + ex_y
        if i == nx - 1:
            hy = hy + up_x[1]
            hz = hz - up_x[0]
            gx_ref[0] = hy
            gx_ref[1] = hz
        out_ref[0, i] = hx
        out_ref[1, i] = hy
        out_ref[2, i] = hz
        gy_ref[0, i : i + 1, :] = hx[15:16]
        gy_ref[1, i : i + 1, :] = hz[15:16]
        for part, value in enumerate((hx, hy)):
            face_z[part] = jnp.where(lane == i, pltpu.roll(value, i + 1, 1), face_z[part])
    for part in range(2):
        gz_ref[part, 0:16, :] = face_z[part]
        gz_ref[part, 16:24, :] = jnp.zeros((8, 128), F32)


def wall_body(decay_ref, gain_ref, poles_ref, e_ref, eps_ref, wall_ref, base_out, slope_out):
    decay = [decay_ref[0:1, p : p + 1] for p in range(poles_ref.shape[0])]
    total = jnp.sum(gain_ref[...], axis=1, keepdims=True)
    for i in range(poles_ref.shape[2]):
        wall = wall_ref[i] == 1
        slope_out[i] = jnp.where(wall, total, 0.5 / eps_ref[i])
        for comp in range(3):
            acc = decay[0] * poles_ref[0, comp, i]
            for p in range(1, poles_ref.shape[0]):
                acc = acc + decay[p] * poles_ref[p, comp, i]
            base_out[comp, i] = jnp.where(wall, acc, e_ref[comp, i])


def elec_body(
    keep, h_ref, dx_ref, dy_ref, dz_ref, base_ref, slope_ref, select_ref, cell_ref, past_ref,
    drive_out, pack_out, cells,
):
    nx = h_ref.shape[1]
    lane = lanes(16, 128)
    row = rows(16, 128)
    dn_x = [dx_ref[part] * keep[3] for part in range(2)]
    dn_y = [dy_ref[part] * keep[4] for part in range(2)]
    dn_z = [dz_ref[part, 0:16, :] * keep[5] for part in range(2)]
    for i in range(nx):
        hx, hy, hz = h_ref[0, i], h_ref[1, i], h_ref[2, i]
        hy_x = h_ref[1, i - 1] if i else dn_x[0]
        hz_x = h_ref[2, i - 1] if i else dn_x[1]
        hx_y = jnp.where(row == 0, dn_y[0][i : i + 1], pltpu.roll(hx, 1, 0))
        hz_y = jnp.where(row == 0, dn_y[1][i : i + 1], pltpu.roll(hz, 1, 0))
        low = [v if i == 0 else pltpu.roll(v, 128 - i, 1) for v in dn_z]
        hx_z = jnp.where(lane == 0, low[0], pltpu.roll(hx, 1, 1))
        hy_z = jnp.where(lane == 0, low[1], pltpu.roll(hy, 1, 1))
        drive = [
            (hz - hz_y) - (hy - hy_z),
            (hx - hx_z) - (hz - hz_x),
            (hy - hy_x) - (hx - hx_y),
        ]
        for comp in range(3):
            drive_out[comp, i] = drive[comp]
        span = pl.ds(i * 16, 16)
        for comp in range(2):
            field = base_ref[comp, i] + slope_ref[i] * drive[comp]
            cells[comp, span, :] = field.astype(BF16)
    packed = past_ref[...] + picked(cells, select_ref[0], cell_ref[0], cell_ref[1])
    packed = packed.astype(BF16)
    pack_out[0] = packed
    pack_out[1] = packed


def picked(cells, select, pick, at):
    lane = lanes(32, 128)
    wide = jnp.zeros((32, 128), F32)
    for e in range(2):
        found = jnp.dot(pick.astype(BF16), cells[e], preferred_element_type=F32)
        value = jnp.sum(found * at, axis=1, keepdims=True)
        wide = jnp.where(lane == 64 * e + 63, value, wide)
    return jnp.dot(select.astype(BF16), wide.astype(BF16), preferred_element_type=F32)


def poles_body(decay_ref, gain_ref, poles_ref, drive_ref, out_ref):
    decay = [decay_ref[0:1, p : p + 1] for p in range(poles_ref.shape[0])]
    gain = [gain_ref[0:1, p : p + 1] for p in range(poles_ref.shape[0])]
    for i in range(poles_ref.shape[2]):
        for comp in range(3):
            drive = drive_ref[comp, i]
            for p in range(poles_ref.shape[0]):
                out_ref[p, comp, i] = decay[p] * poles_ref[p, comp, i] + gain[p] * drive


def field_body(drive_ref, base_ref, slope_ref, h_ref, e_out, h_out):
    h_out[...] = h_ref[...]
    for comp in range(3):
        e_out[comp] = base_ref[comp] + slope_ref[...] * drive_ref[comp]


def pack_body(owner_ref, cell_ref, hist_ref, h_ref, select_out, cell_out, pack_out, cells):
    for comp in range(2):
        for i in range(h_ref.shape[1]):
            cells[comp, i * 16 : (i + 1) * 16, :] = h_ref[comp, i].astype(BF16)
    owner = owner_ref[...]
    onehot = jnp.where(rows(16, 32) == owner, 1.0, 0.0)
    earlier = jnp.where(rows(32, 32) < lanes(32, 32), 1.0, 0.0).astype(BF16)
    count = jnp.dot(onehot.astype(BF16), earlier, preferred_element_type=F32)
    rank = jnp.sum(count * onehot, axis=0, keepdims=True).astype(jnp.int32)
    slot = owner * 8 + rank
    cell = cell_ref[...]
    row = rows(128, 32)
    pick = jnp.where(row == (cell >> 7), 1.0, 0.0).T
    at = jnp.where(row == (cell & 127), 1.0, 0.0).T
    cell_out[0] = pick
    cell_out[1] = at
    packed = jnp.zeros((128, 128), F32)
    for half in range(2):
        select = jnp.where(row == slot + 4 * half, 1.0, 0.0)
        select_out[half] = select
        gap = jnp.zeros((32, 1), F32)
        past = [hist_ref[2 * half + e].astype(F32) for e in range(2)]
        past = jnp.concatenate([past[0], gap, past[1], gap], axis=1)
        packed = packed + jnp.dot(
            select.astype(BF16), past.astype(BF16), preferred_element_type=F32
        )
    pack_out[...] = packed + picked(cells, select, pick, at)


def beside(first, second):
    low = lanes(*first.shape) < 64
    return (
        jnp.where(low, first, pltpu.roll(second, 64, 1)),
        jnp.where(low, pltpu.roll(first, 64, 1), second),
    )


def project_body(core, got_ref, steer_ref, series_out, out_ref):
    got = got_ref[...]
    row, slot = rows(256, 128), lanes(256, 128)
    parts = []
    for half in range(2):
        place = jnp.where(row == (slot >> 2) * 8 + 4 * half + (slot & 3), 1.0, 0.0).astype(BF16)
        moved = dot_t(got, place).astype(BF16)
        parts += [moved[:64], moved[64:]]
    series = jnp.concatenate(parts, axis=1)
    series_out[...] = series
    project_half(1 - core[0], series, steer_ref, out_ref, None)


def project_half(half, series, steer_ref, out_ref, add_ref):
    for n in range(4):
        first = pl.multiple_of(half * 1024 + n * 256, 256)
        part = jnp.dot(series, steer_ref[:, pl.ds(first, 256)], preferred_element_type=F32)
        for m in range(2):
            pair = beside(part[:32, m * 128 : (m + 1) * 128], part[32:, m * 128 : (m + 1) * 128])
            for y in range(2):
                at = 4 * n + 2 * m + y
                out_ref[at] = pair[y] if add_ref is None else pair[y] + add_ref[at]


def project_own_body(core, series_ref, steer_ref, add_ref, out_ref):
    project_half(core[0], series_ref[...], steer_ref, out_ref, add_ref)


def sum_body(got_ref, out_ref):
    total = got_ref[0]
    for a in range(1, got_ref.shape[0]):
        total = total + got_ref[a]
    out_ref[...] = total


def spectrum_body(core, mine_ref, other_ref, table_ref, out_ref):
    mine, other = mine_ref[...], other_ref[...]
    first = core[0] == 0
    both = beside(jnp.where(first, mine, other), jnp.where(first, other, mine))
    both = jnp.concatenate(both, axis=0)
    high = both.astype(BF16)
    low = (both - high.astype(F32)).astype(BF16)
    out_ref[...] = jnp.dot(
        table_ref[core[0]], jnp.concatenate([high, low, high], axis=0), preferred_element_type=F32
    )


def finish_body(got_ref, out_ref):
    total = [got_ref[32 * y : 32 * y + 32, :] for y in range(2)]
    for b in range(1, 4):
        total = [total[y] + got_ref[64 * b + 32 * y : 64 * b + 32 * y + 32, :] for y in range(2)]
    for core, value in enumerate(beside(*total)):
        for g in range(8):
            first = (8 * core + g) * 128
            for s in range(2):
                at = 4 * g + 2 * s
                out_ref[s, :, first : first + 128] = value[at : at + 2]


def spectral_table(steps):
    times = np.arange(steps, dtype=np.float64)
    levels = np.arange(FREQS, dtype=np.float64) + 0.5
    phase = math.pi / (2.0 * FREQS) * levels[:, None] * times[None, :]
    table = np.stack([np.cos(phase), -np.sin(phase)]) / math.sqrt(steps)
    return table.astype(np.float32)


def peer_table(steps):
    table = spectral_table(steps).reshape(2, 8, 2, 8, 2, steps).transpose(2, 3, 1, 0, 4, 5)
    table = table.reshape(2, 256, steps)
    high = table.astype(jnp.bfloat16)
    low = (table - high.astype(np.float32)).astype(jnp.bfloat16)
    return jnp.asarray(np.concatenate([high, high, low], axis=2))


def shift(value, axis, step):
    count = lax.axis_size(axis)
    return lax.ppermute(value, axis, [(i, (i + step) % count) for i in range(count)])


def cross(sender):
    pairs, count = [], lax.axis_size("gxc")
    for g in range(count):
        near = (g + count // 2) % count
        pairs += [(2 * g + sender, 2 * g + 1 - sender), (2 * g + 1 - sender, 2 * near + sender)]
    return pairs


def per_device(
    e_field, h_field, permittivity, wall_mask, poles, pole_decay, pole_gain, face_cells, owners,
    history, steering,
):
    nx, ny, nz = e_field.shape[1:]
    steps = history.shape[0] + 1
    axes = (GX, GY, "gz")
    places = [lax.axis_index(axis) for axis in axes]
    keep = jnp.stack(
        [(at < lax.axis_size(axis) - 1) for at, axis in zip(places, axes)]
        + [at > 0 for at in places]
    ).astype(F32)
    core = lax.axis_index("core").reshape(1)
    block = struct(3, nx, ny, nz)
    faces = [struct(2, ny, nz), struct(2, 4 * nx, nz), struct(2, ny + 8, 128)]
    faces_up = [struct(2, ny, nz), struct(2, nx, nz), struct(2, ny + 8, 128)]

    *near, e_near, h_near = call(
        face_body, [*faces, block, block], [HB] * 2, [pltpu.SemaphoreType.DMA((2,))], data=400000
    )(far_off(e_field), far_off(h_field))
    up = [shift(face, axis, -1) for face, axis in zip(near[:2], axes)]
    up.append(lax.ppermute(near[2], ("gxc", "gz"), cross(1)))
    near, e_near, h_near = lax.optimization_barrier((near, e_near, h_near))
    later = [
        poles, permittivity, wall_mask, pole_decay.reshape(1, -1), pole_gain.reshape(1, -1),
        owners.reshape(1, -1), face_cells.reshape(1, -1), jnp.transpose(history, (1, 2, 0)),
    ]
    inner, poles, permittivity, wall_mask, decay, gain, owners, face_cells, history = call(
        inner_body,
        [block, *[struct(*value.shape, dtype=value.dtype) for value in later]],
        [VM] * 2 + [HB] * len(later),
        [pltpu.SemaphoreType.DMA((len(later),))],
        data=2600000,
    )(e_near, h_near, *[far_off(value) for value in later])

    h_mid, *far = call(mag_body, [block, *faces_up], [SM] + [VM] * 4, data=500000)(keep, inner, *up)
    down = [shift(face, axis, 1) for face, axis in zip(far[:2], axes)]
    down.append(lax.ppermute(far[2], ("gxc", "gz"), cross(0)))
    far, owners, poles = lax.optimization_barrier((far, owners, poles))
    select, cell, leaving = call(
        pack_body,
        [struct(2, 128, 32), struct(2, 32, 128), struct(128, 128)],
        [VM] * 4,
        scratch=[pltpu.VMEM((2, 128, 128), BF16)],
        data=200000,
    )(owners, face_cells, history, h_mid)
    base, slope = call(wall_body, [block, struct(nx, ny, nz)], [VM] * 6, data=2400000)(
        decay, gain, poles, e_near, permittivity, wall_mask
    )

    drive, leaving = call(
        elec_body,
        [block, struct(2, 128, 128, dtype=BF16)],
        [SM] + [VM] * 9,
        scratch=[pltpu.VMEM((2, 128, 128), BF16)],
        data=1200000,
    )(keep, h_mid, *down, base, slope, select, cell, leaving)
    arrived = lax.all_to_all(leaving.reshape(32, 8, 128), ("gz", *GX), 0, 0, tiled=True)
    poles_next = call(poles_body, struct(*poles.shape), [VM] * 4, data=3400000)(
        decay, gain, poles, drive
    )
    e_next, h_next = call(field_body, [block, block], [VM] * 4, data=1200000)(
        drive, base, slope, h_mid
    )

    weights = steering.reshape(-1, steering.shape[2])
    series, part = call(
        project_body,
        [struct(64, 512, dtype=BF16), struct(16, 32, 128)],
        [SM] + [VM] * 2,
        flops=1 << 26,
        data=2600000,
    )(core, arrived.reshape(256, 128), weights)
    part = lax.ppermute(part, "core", [(0, 1), (1, 0)])
    series, poles_next = lax.optimization_barrier((series, poles_next))
    part = call(project_own_body, struct(16, 32, 128), [SM] + [VM] * 3, flops=1 << 26, data=2600000)(
        core, series, weights, part
    )
    part = lax.all_to_all(part, ("gxc", "gyl"), 0, 0, tiled=True)
    mine = call(sum_body, struct(32, 128), [VM], data=300000)(part)
    other = lax.ppermute(mine, "core", [(0, 1), (1, 0)])
    core, e_next = lax.optimization_barrier((core, e_next))
    spectra = call(spectrum_body, struct(256, 128), [SM] + [VM] * 3, flops=1 << 27, data=900000)(
        core, mine, other, peer_table(steps)
    )
    spectra = lax.all_to_all(spectra, (*GY, "gxc"), 0, 0, tiled=True)
    far_field = call(finish_body, struct(2, 2, 2048), [VM], data=300000)(spectra)
    return (e_next, h_next, poles_next, far_field)


GX = ("gxc", "core")
GY = ("gyh", "gyl")


def solution(mesh):
    shape = (mesh.shape["gx"] // 2, 2, mesh.shape["gy"] // 2, 2, mesh.shape["gz"])
    mesh = jax.sharding.Mesh(mesh.devices.reshape(shape), (*GX, *GY, "gz"))
    return jax.shard_map(
        per_device,
        mesh=mesh,
        in_specs=(
            P(None, GX, GY, "gz"),
            P(None, GX, GY, "gz"),
            P(GX, GY, "gz"),
            P(GX, GY, "gz"),
            P(None, None, GX, GY, "gz"),
            P(),
            P(),
            P((*GX, *GY, "gz")),
            P((*GX, *GY, "gz"), None),
            P(None, None, (*GX, *GY, "gz")),
            P(None, (*GX, *GY), "gz"),
        ),
        out_specs=(
            P(None, GX, GY, "gz"),
            P(None, GX, GY, "gz"),
            P(None, None, GX, GY, "gz"),
            P(None, (*GX, *GY), "gz"),
        ),
        check_vma=False,
    )
```

```python
import math

import jax
import jax.numpy as jnp
import numpy as np
from jax import lax
from jax.experimental import pallas as pl
from jax.experimental.pallas import tpu as pltpu
from jax.sharding import PartitionSpec as P

FREQS = 256
F32 = jnp.float32
BF16 = jnp.bfloat16
VM = pl.BlockSpec(memory_space=pltpu.VMEM)
SM = pl.BlockSpec(memory_space=pltpu.SMEM)
HB = pl.BlockSpec(memory_space=pltpu.HBM)


def call(body, out_shape, in_specs, scratch=(), flops=0, data=0):
    many = isinstance(out_shape, (list, tuple))
    return pl.pallas_call(
        body,
        out_shape=out_shape,
        in_specs=in_specs,
        out_specs=[VM] * len(out_shape) if many else VM,
        scratch_shapes=list(scratch),
        compiler_params=pltpu.CompilerParams(vmem_limit_bytes=32 << 20),
        cost_estimate=pl.CostEstimate(flops=flops, bytes_accessed=data, transcendentals=0),
    )


def far_off(value):
    return pltpu.with_memory_space_constraint(value, pltpu.HBM)


def struct(*shape, dtype=F32):
    return jax.ShapeDtypeStruct(shape, dtype)


def lanes(*shape):
    return lax.broadcasted_iota(jnp.int32, shape, len(shape) - 1)


def rows(*shape):
    return lax.broadcasted_iota(jnp.int32, shape, len(shape) - 2)


def dot_t(a, b):
    return lax.dot_general(a, b, (((0,), (0,)), ((), ())), preferred_element_type=F32)


def fetch(pairs, sems):
    copies = [pltpu.make_async_copy(*pair, sems.at[n]) for n, pair in enumerate(pairs)]
    for copy in copies:
        copy.start()
    return copies


def face_body(e_far, h_far, fx_ref, fy_ref, fz_ref, e_ref, h_ref, sems):
    bring = fetch([(e_far, e_ref), (h_far, h_ref)], sems)
    bring[0].wait()
    nx = e_ref.shape[1]
    fx_ref[0] = e_ref[1, 0]
    fx_ref[1] = e_ref[2, 0]
    lane = lanes(16, 128)
    fy_ref[...] = jnp.zeros_like(fy_ref)
    for part, comp in enumerate((0, 2)):
        for i in range(nx):
            fy_ref[part, i : i + 1, :] = e_ref[comp, i, 0:1, :]
    for part, comp in enumerate((0, 1)):
        acc = jnp.zeros((16, 128), F32)
        for i in range(nx):
            moved = e_ref[comp, i] if i == 0 else pltpu.roll(e_ref[comp, i], i, 1)
            acc = jnp.where(lane == i, moved, acc)
        fz_ref[part, 0:16, :] = acc
        fz_ref[part, 16:24, :] = jnp.zeros((8, 128), F32)
    bring[1].wait()


def inner_body(e_ref, h_ref, *refs):
    count = (len(refs) - 2) // 2
    out_ref, sems = refs[count], refs[-1]
    bring = fetch(list(zip(refs[:count], refs[count + 1 : -1])), sems)
    nx = e_ref.shape[1]
    lane = lanes(16, 128)
    row = rows(16, 128)
    zero = jnp.zeros((16, 128), F32)
    for i in range(nx):
        ex, ey, ez = e_ref[0, i], e_ref[1, i], e_ref[2, i]
        ey_x = e_ref[1, i + 1] if i + 1 < nx else zero
        ez_x = e_ref[2, i + 1] if i + 1 < nx else zero
        ex_y = jnp.where(row == 15, 0.0, pltpu.roll(ex, 15, 0))
        ez_y = jnp.where(row == 15, 0.0, pltpu.roll(ez, 15, 0))
        ex_z = jnp.where(lane == 127, 0.0, pltpu.roll(ex, 127, 1))
        ey_z = jnp.where(lane == 127, 0.0, pltpu.roll(ey, 127, 1))
        out_ref[0, i] = h_ref[0, i] - 0.5 * ((ez_y - ez) - (ey_z - ey))
        out_ref[1, i] = h_ref[1, i] - 0.5 * ((ex_z - ex) - (ez_x - ez))
        out_ref[2, i] = h_ref[2, i] - 0.5 * ((ey_x - ey) - (ex_y - ex))
    for copy in bring:
        copy.wait()


def upper_terms(keep, ux_ref, uy_ref, uz_ref):
    lane, row = lanes(16, 128), rows(16, 128)
    up_x = [ux_ref[part] * (0.5 * keep[0]) for part in range(2)]
    up_y = [uy_ref[part] * (0.5 * keep[1]) for part in range(2)]
    up_z = [uz_ref[part, 0:16, :] * (0.5 * keep[2]) for part in range(2)]

    def whole(part_ref, i):
        ex_z, ey_z = [jnp.where(lane == 127, pltpu.roll(v, 127 - i, 1), 0.0) for v in up_z]
        ex_y, ez_y = [jnp.where(row == 15, v[i : i + 1], 0.0) for v in up_y]
        hx = part_ref[0, i] + (ey_z - ez_y)
        hy = part_ref[1, i] - ex_z
        hz = part_ref[2, i] + ex_y
        if i == part_ref.shape[1] - 1:
            hy = hy + up_x[1]
            hz = hz - up_x[0]
        return hx, hy, hz

    return whole


def edge_body(keep, part_ref, ux_ref, uy_ref, uz_ref, gx_ref, gy_ref, gz_ref):
    nx = part_ref.shape[1]
    lane = lanes(16, 128)
    whole = upper_terms(keep, ux_ref, uy_ref, uz_ref)
    face_z = [jnp.zeros((16, 128), F32), jnp.zeros((16, 128), F32)]
    for i in range(nx):
        hx, hy, hz = whole(part_ref, i)
        if i == nx - 1:
            gx_ref[0] = hy
            gx_ref[1] = hz
        gy_ref[0, i : i + 1, :] = hx[15:16]
        gy_ref[1, i : i + 1, :] = hz[15:16]
        for part, value in enumerate((hx, hy)):
            face_z[part] = jnp.where(lane == i, pltpu.roll(value, i + 1, 1), face_z[part])
    for part in range(2):
        gz_ref[part, 0:16, :] = face_z[part]
        gz_ref[part, 16:24, :] = jnp.zeros((8, 128), F32)


def mag_body(keep, part_ref, ux_ref, uy_ref, uz_ref, out_ref, drive_ref):
    lane, row = lanes(16, 128), rows(16, 128)
    whole = upper_terms(keep, ux_ref, uy_ref, uz_ref)
    hy_x = hz_x = jnp.zeros((16, 128), F32)
    for i in range(part_ref.shape[1]):
        hx, hy, hz = whole(part_ref, i)
        out_ref[0, i] = hx
        out_ref[1, i] = hy
        out_ref[2, i] = hz
        hx_y, hz_y = [jnp.where(row == 0, 0.0, pltpu.roll(v, 1, 0)) for v in (hx, hz)]
        hx_z, hy_z = [jnp.where(lane == 0, 0.0, pltpu.roll(v, 1, 1)) for v in (hx, hy)]
        drive_ref[0, i] = (hz - hz_y) - (hy - hy_z)
        drive_ref[1, i] = (hx - hx_z) - (hz - hz_x)
        drive_ref[2, i] = (hy - hy_x) - (hx - hx_y)
        hy_x, hz_x = hy, hz


def wall_body(decay_ref, gain_ref, poles_ref, e_ref, eps_ref, wall_ref, base_out, slope_out):
    decay = [decay_ref[0:1, p : p + 1] for p in range(poles_ref.shape[0])]
    total = jnp.sum(gain_ref[...], axis=1, keepdims=True)
    for i in range(poles_ref.shape[2]):
        wall = wall_ref[i] == 1
        slope_out[i] = jnp.where(wall, total, 0.5 / eps_ref[i])
        for comp in range(3):
            acc = decay[0] * poles_ref[0, comp, i]
            for p in range(1, poles_ref.shape[0]):
                acc = acc + decay[p] * poles_ref[p, comp, i]
            base_out[comp, i] = jnp.where(wall, acc, e_ref[comp, i])


def elec_body(
    keep, part_ref, dx_ref, dy_ref, dz_ref, base_ref, slope_ref, select_ref, cell_ref, past_ref,
    drive_out, pack_out, cells,
):
    nx = part_ref.shape[1]
    lane = lanes(16, 128)
    row = rows(16, 128)
    dn_x = [dx_ref[part] * keep[3] for part in range(2)]
    dn_y = [dy_ref[part] * keep[4] for part in range(2)]
    dn_z = [dz_ref[part, 0:16, :] * keep[5] for part in range(2)]
    for i in range(nx):
        low = [v if i == 0 else pltpu.roll(v, 128 - i, 1) for v in dn_z]
        hx_z, hy_z = [jnp.where(lane == 0, v, 0.0) for v in low]
        hx_y, hz_y = [jnp.where(row == 0, v[i : i + 1], 0.0) for v in dn_y]
        drive = [
            part_ref[0, i] + (hy_z - hz_y),
            part_ref[1, i] - hx_z,
            part_ref[2, i] + hx_y,
        ]
        if i == 0:
            drive[1] = drive[1] + dn_x[1]
            drive[2] = drive[2] - dn_x[0]
        for comp in range(3):
            drive_out[comp, i] = drive[comp]
        span = pl.ds(i * 16, 16)
        for comp in range(2):
            field = base_ref[comp, i] + slope_ref[i] * drive[comp]
            cells[comp, span, :] = field.astype(BF16)
    packed = past_ref[...] + picked(cells, select_ref[0], cell_ref[0], cell_ref[1])
    packed = packed.astype(BF16)
    pack_out[0] = packed
    pack_out[1] = packed


def picked(cells, select, pick, at):
    lane = lanes(32, 128)
    wide = jnp.zeros((32, 128), F32)
    for e in range(2):
        found = jnp.dot(pick.astype(BF16), cells[e], preferred_element_type=F32)
        value = jnp.sum(found * at, axis=1, keepdims=True)
        wide = jnp.where(lane == 64 * e + 63, value, wide)
    return jnp.dot(select.astype(BF16), wide.astype(BF16), preferred_element_type=F32)


def poles_body(decay_ref, gain_ref, poles_ref, drive_ref, out_ref):
    decay = [decay_ref[0:1, p : p + 1] for p in range(poles_ref.shape[0])]
    gain = [gain_ref[0:1, p : p + 1] for p in range(poles_ref.shape[0])]
    for i in range(poles_ref.shape[2]):
        for comp in range(3):
            drive = drive_ref[comp, i]
            for p in range(poles_ref.shape[0]):
                out_ref[p, comp, i] = decay[p] * poles_ref[p, comp, i] + gain[p] * drive


def field_body(drive_ref, base_ref, slope_ref, h_ref, e_out, h_out):
    h_out[...] = h_ref[...]
    for comp in range(3):
        e_out[comp] = base_ref[comp] + slope_ref[...] * drive_ref[comp]


def pack_body(owner_ref, cell_ref, hist_ref, h_ref, select_out, cell_out, pack_out, cells):
    for comp in range(2):
        for i in range(h_ref.shape[1]):
            cells[comp, i * 16 : (i + 1) * 16, :] = h_ref[comp, i].astype(BF16)
    owner = owner_ref[...]
    onehot = jnp.where(rows(16, 32) == owner, 1.0, 0.0)
    earlier = jnp.where(rows(32, 32) < lanes(32, 32), 1.0, 0.0).astype(BF16)
    count = jnp.dot(onehot.astype(BF16), earlier, preferred_element_type=F32)
    rank = jnp.sum(count * onehot, axis=0, keepdims=True).astype(jnp.int32)
    slot = owner * 8 + rank
    cell = cell_ref[...]
    row = rows(128, 32)
    pick = jnp.where(row == (cell >> 7), 1.0, 0.0).T
    at = jnp.where(row == (cell & 127), 1.0, 0.0).T
    cell_out[0] = pick
    cell_out[1] = at
    packed = jnp.zeros((128, 128), F32)
    for half in range(2):
        select = jnp.where(row == slot + 4 * half, 1.0, 0.0)
        select_out[half] = select
        gap = jnp.zeros((32, 1), F32)
        past = [hist_ref[2 * half + e].astype(F32) for e in range(2)]
        past = jnp.concatenate([past[0], gap, past[1], gap], axis=1)
        packed = packed + jnp.dot(
            select.astype(BF16), past.astype(BF16), preferred_element_type=F32
        )
    pack_out[...] = packed + picked(cells, select, pick, at)


def beside(first, second):
    low = lanes(*first.shape) < 64
    return (
        jnp.where(low, first, pltpu.roll(second, 64, 1)),
        jnp.where(low, pltpu.roll(first, 64, 1), second),
    )


def project_body(core, got_ref, steer_ref, series_out, out_ref):
    got = got_ref[...]
    row, slot = rows(256, 128), lanes(256, 128)
    parts = []
    for half in range(2):
        place = jnp.where(row == (slot >> 2) * 8 + 4 * half + (slot & 3), 1.0, 0.0).astype(BF16)
        moved = dot_t(got, place).astype(BF16)
        parts += [moved[:64], moved[64:]]
    series = jnp.concatenate(parts, axis=1)
    series_out[...] = series
    project_half(1 - core[0], series, steer_ref, out_ref, None)


def project_half(half, series, steer_ref, out_ref, add_ref):
    for n in range(4):
        first = pl.multiple_of(half * 1024 + n * 256, 256)
        part = jnp.dot(series, steer_ref[:, pl.ds(first, 256)], preferred_element_type=F32)
        for m in range(2):
            pair = beside(part[:32, m * 128 : (m + 1) * 128], part[32:, m * 128 : (m + 1) * 128])
            for y in range(2):
                at = 4 * n + 2 * m + y
                out_ref[at] = pair[y] if add_ref is None else pair[y] + add_ref[at]


def project_own_body(core, series_ref, steer_ref, add_ref, out_ref):
    project_half(core[0], series_ref[...], steer_ref, out_ref, add_ref)


def sum_body(got_ref, out_ref):
    total = got_ref[0]
    for a in range(1, got_ref.shape[0]):
        total = total + got_ref[a]
    out_ref[...] = total


def spectrum_body(core, mine_ref, other_ref, table_ref, out_ref):
    mine, other = mine_ref[...], other_ref[...]
    first = core[0] == 0
    both = beside(jnp.where(first, mine, other), jnp.where(first, other, mine))
    both = jnp.concatenate(both, axis=0)
    high = both.astype(BF16)
    low = (both - high.astype(F32)).astype(BF16)
    out_ref[...] = jnp.dot(
        table_ref[core[0]], jnp.concatenate([high, low, high], axis=0), preferred_element_type=F32
    )


def finish_body(got_ref, out_ref):
    total = [got_ref[32 * y : 32 * y + 32, :] for y in range(2)]
    for b in range(1, 4):
        total = [total[y] + got_ref[64 * b + 32 * y : 64 * b + 32 * y + 32, :] for y in range(2)]
    for core, value in enumerate(beside(*total)):
        for g in range(8):
            first = (8 * core + g) * 128
            for s in range(2):
                at = 4 * g + 2 * s
                out_ref[s, :, first : first + 128] = value[at : at + 2]


def spectral_table(steps):
    times = np.arange(steps, dtype=np.float64)
    levels = np.arange(FREQS, dtype=np.float64) + 0.5
    phase = math.pi / (2.0 * FREQS) * levels[:, None] * times[None, :]
    table = np.stack([np.cos(phase), -np.sin(phase)]) / math.sqrt(steps)
    return table.astype(np.float32)


def peer_table(steps):
    table = spectral_table(steps).reshape(2, 8, 2, 8, 2, steps).transpose(2, 3, 1, 0, 4, 5)
    table = table.reshape(2, 256, steps)
    high = table.astype(jnp.bfloat16)
    low = (table - high.astype(np.float32)).astype(jnp.bfloat16)
    return jnp.asarray(np.concatenate([high, high, low], axis=2))


def shift(value, axis, step):
    count = lax.axis_size(axis)
    return lax.ppermute(value, axis, [(i, (i + step) % count) for i in range(count)])


def cross(sender):
    pairs, count = [], lax.axis_size("gxc")
    for g in range(count):
        near = (g + count // 2) % count
        pairs += [(2 * g + sender, 2 * g + 1 - sender), (2 * g + 1 - sender, 2 * near + sender)]
    return pairs


def per_device(
    e_field, h_field, permittivity, wall_mask, poles, pole_decay, pole_gain, face_cells, owners,
    history, steering,
):
    nx, ny, nz = e_field.shape[1:]
    steps = history.shape[0] + 1
    axes = (GX, GY, "gz")
    places = [lax.axis_index(axis) for axis in axes]
    keep = jnp.stack(
        [(at < lax.axis_size(axis) - 1) for at, axis in zip(places, axes)]
        + [at > 0 for at in places]
    ).astype(F32)
    core = lax.axis_index("core").reshape(1)
    block = struct(3, nx, ny, nz)
    faces = [struct(2, ny, nz), struct(2, 4 * nx, nz), struct(2, ny + 8, 128)]
    faces_up = [struct(2, ny, nz), struct(2, nx, nz), struct(2, ny + 8, 128)]

    *near, e_near, h_near = call(
        face_body, [*faces, block, block], [HB] * 2, [pltpu.SemaphoreType.DMA((2,))], data=400000
    )(far_off(e_field), far_off(h_field))
    up = [shift(face, axis, -1) for face, axis in zip(near[:2], axes)]
    up.append(lax.ppermute(near[2], ("gxc", "gz"), cross(1)))
    near, e_near, h_near = lax.optimization_barrier((near, e_near, h_near))
    later = [
        poles, permittivity, wall_mask, pole_decay.reshape(1, -1), pole_gain.reshape(1, -1),
        owners.reshape(1, -1), face_cells.reshape(1, -1), jnp.transpose(history, (1, 2, 0)),
    ]
    inner, poles, permittivity, wall_mask, decay, gain, owners, face_cells, history = call(
        inner_body,
        [block, *[struct(*value.shape, dtype=value.dtype) for value in later]],
        [VM] * 2 + [HB] * len(later),
        [pltpu.SemaphoreType.DMA((len(later),))],
        data=2600000,
    )(e_near, h_near, *[far_off(value) for value in later])

    far = call(edge_body, faces_up, [SM] + [VM] * 4, data=500000)(keep, inner, *up)
    down = [shift(face, axis, 1) for face, axis in zip(far[:2], axes)]
    down.append(lax.ppermute(far[2], ("gxc", "gz"), cross(0)))
    far, owners, poles, inner = lax.optimization_barrier((far, owners, poles, inner))
    h_mid, part = call(mag_body, [block, block], [SM] + [VM] * 4, data=500000)(keep, inner, *up)
    select, cell, leaving = call(
        pack_body,
        [struct(2, 128, 32), struct(2, 32, 128), struct(128, 128)],
        [VM] * 4,
        scratch=[pltpu.VMEM((2, 128, 128), BF16)],
        data=200000,
    )(owners, face_cells, history, h_mid)
    base, slope = call(wall_body, [block, struct(nx, ny, nz)], [VM] * 6, data=2400000)(
        decay, gain, poles, e_near, permittivity, wall_mask
    )

    drive, leaving = call(
        elec_body,
        [block, struct(2, 128, 128, dtype=BF16)],
        [SM] + [VM] * 9,
        scratch=[pltpu.VMEM((2, 128, 128), BF16)],
        data=1200000,
    )(keep, part, *down, base, slope, select, cell, leaving)
    arrived = lax.all_to_all(leaving.reshape(32, 8, 128), ("gz", *GX), 0, 0, tiled=True)
    poles_next = call(poles_body, struct(*poles.shape), [VM] * 4, data=3400000)(
        decay, gain, poles, drive
    )
    e_next, h_next = call(field_body, [block, block], [VM] * 4, data=1200000)(
        drive, base, slope, h_mid
    )

    weights = steering.reshape(-1, steering.shape[2])
    series, part = call(
        project_body,
        [struct(64, 512, dtype=BF16), struct(16, 32, 128)],
        [SM] + [VM] * 2,
        flops=1 << 26,
        data=2600000,
    )(core, arrived.reshape(256, 128), weights)
    part = lax.ppermute(part, "core", [(0, 1), (1, 0)])
    series, poles_next = lax.optimization_barrier((series, poles_next))
    part = call(project_own_body, struct(16, 32, 128), [SM] + [VM] * 3, flops=1 << 26, data=2600000)(
        core, series, weights, part
    )
    part = lax.all_to_all(part, ("gxc", "gyl"), 0, 0, tiled=True)
    mine = call(sum_body, struct(32, 128), [VM], data=300000)(part)
    other = lax.ppermute(mine, "core", [(0, 1), (1, 0)])
    core, e_next = lax.optimization_barrier((core, e_next))
    spectra = call(spectrum_body, struct(256, 128), [SM] + [VM] * 3, flops=1 << 27, data=900000)(
        core, mine, other, peer_table(steps)
    )
    spectra = lax.all_to_all(spectra, (*GY, "gxc"), 0, 0, tiled=True)
    far_field = call(finish_body, struct(2, 2, 2048), [VM], data=300000)(spectra)
    return (e_next, h_next, poles_next, far_field)


GX = ("gxc", "core")
GY = ("gyh", "gyl")


def solution(mesh):
    shape = (mesh.shape["gx"] // 2, 2, mesh.shape["gy"] // 2, 2, mesh.shape["gz"])
    mesh = jax.sharding.Mesh(mesh.devices.reshape(shape), (*GX, *GY, "gz"))
    return jax.shard_map(
        per_device,
        mesh=mesh,
        in_specs=(
            P(None, GX, GY, "gz"),
            P(None, GX, GY, "gz"),
            P(GX, GY, "gz"),
            P(GX, GY, "gz"),
            P(None, None, GX, GY, "gz"),
            P(),
            P(),
            P((*GX, *GY, "gz")),
            P((*GX, *GY, "gz"), None),
            P(None, None, (*GX, *GY, "gz")),
            P(None, (*GX, *GY), "gz"),
        ),
        out_specs=(
            P(None, GX, GY, "gz"),
            P(None, GX, GY, "gz"),
            P(None, None, GX, GY, "gz"),
            P(None, (*GX, *GY), "gz"),
        ),
        check_vma=False,
    )
```

```python
import math

import jax
import jax.numpy as jnp
import numpy as np
from jax import lax
from jax.experimental import pallas as pl
from jax.experimental.pallas import tpu as pltpu
from jax.sharding import PartitionSpec as P

FREQS = 256
F32 = jnp.float32
BF16 = jnp.bfloat16
VM = pl.BlockSpec(memory_space=pltpu.VMEM)
SM = pl.BlockSpec(memory_space=pltpu.SMEM)
HB = pl.BlockSpec(memory_space=pltpu.HBM)


def call(body, out_shape, in_specs, scratch=(), flops=0, data=0):
    many = isinstance(out_shape, (list, tuple))
    return pl.pallas_call(
        body,
        out_shape=out_shape,
        in_specs=in_specs,
        out_specs=[VM] * len(out_shape) if many else VM,
        scratch_shapes=list(scratch),
        compiler_params=pltpu.CompilerParams(vmem_limit_bytes=32 << 20),
        cost_estimate=pl.CostEstimate(flops=flops, bytes_accessed=data, transcendentals=0),
    )


def far_off(value):
    return pltpu.with_memory_space_constraint(value, pltpu.HBM)


def struct(*shape, dtype=F32):
    return jax.ShapeDtypeStruct(shape, dtype)


def lanes(*shape):
    return lax.broadcasted_iota(jnp.int32, shape, len(shape) - 1)


def rows(*shape):
    return lax.broadcasted_iota(jnp.int32, shape, len(shape) - 2)


def dot_t(a, b):
    return lax.dot_general(a, b, (((0,), (0,)), ((), ())), preferred_element_type=F32)


def fetch(pairs, sems):
    copies = [pltpu.make_async_copy(*pair, sems.at[n]) for n, pair in enumerate(pairs)]
    for copy in copies:
        copy.start()
    return copies


def face_body(e_far, h_far, fx_ref, fy_ref, fz_ref, e_ref, h_ref, sems):
    bring = fetch([(e_far, e_ref), (h_far, h_ref)], sems)
    bring[0].wait()
    nx = e_ref.shape[1]
    fx_ref[0] = e_ref[1, 0]
    fx_ref[1] = e_ref[2, 0]
    lane = lanes(16, 128)
    fy_ref[...] = jnp.zeros_like(fy_ref)
    for part, comp in enumerate((0, 2)):
        for i in range(nx):
            fy_ref[part, i : i + 1, :] = e_ref[comp, i, 0:1, :]
    for part, comp in enumerate((0, 1)):
        acc = jnp.zeros((16, 128), F32)
        for i in range(nx):
            moved = e_ref[comp, i] if i == 0 else pltpu.roll(e_ref[comp, i], i, 1)
            acc = jnp.where(lane == i, moved, acc)
        fz_ref[part, 0:16, :] = acc
        fz_ref[part, 16:24, :] = jnp.zeros((8, 128), F32)
    bring[1].wait()


def inner_body(e_ref, h_ref, *refs):
    count = (len(refs) - 2) // 2
    out_ref, sems = refs[count], refs[-1]
    bring = fetch(list(zip(refs[:count], refs[count + 1 : -1])), sems)
    nx = e_ref.shape[1]
    lane = lanes(16, 128)
    row = rows(16, 128)
    zero = jnp.zeros((16, 128), F32)
    for i in range(nx):
        ex, ey, ez = e_ref[0, i], e_ref[1, i], e_ref[2, i]
        ey_x = e_ref[1, i + 1] if i + 1 < nx else zero
        ez_x = e_ref[2, i + 1] if i + 1 < nx else zero
        ex_y = jnp.where(row == 15, 0.0, pltpu.roll(ex, 15, 0))
        ez_y = jnp.where(row == 15, 0.0, pltpu.roll(ez, 15, 0))
        ex_z = jnp.where(lane == 127, 0.0, pltpu.roll(ex, 127, 1))
        ey_z = jnp.where(lane == 127, 0.0, pltpu.roll(ey, 127, 1))
        out_ref[0, i] = h_ref[0, i] - 0.5 * ((ez_y - ez) - (ey_z - ey))
        out_ref[1, i] = h_ref[1, i] - 0.5 * ((ex_z - ex) - (ez_x - ez))
        out_ref[2, i] = h_ref[2, i] - 0.5 * ((ey_x - ey) - (ex_y - ex))
    for copy in bring:
        copy.wait()


def upper_terms(keep_ref, ux_ref, uy_ref, uz_ref):
    lane, row = lanes(16, 128), rows(16, 128)
    up_x = [ux_ref[part] * (0.5 * keep_ref[0 : 0 + 1, :]) for part in range(2)]
    up_y = [uy_ref[part] * (0.5 * keep_ref[1 : 1 + 1, :]) for part in range(2)]
    up_z = [uz_ref[part, 0:16, :] * (0.5 * keep_ref[2 : 2 + 1, :]) for part in range(2)]

    def whole(part_ref, i):
        ex_z, ey_z = [jnp.where(lane == 127, pltpu.roll(v, 127 - i, 1), 0.0) for v in up_z]
        ex_y, ez_y = [jnp.where(row == 15, v[i : i + 1], 0.0) for v in up_y]
        hx = part_ref[0, i] + (ey_z - ez_y)
        hy = part_ref[1, i] - ex_z
        hz = part_ref[2, i] + ex_y
        if i == part_ref.shape[1] - 1:
            hy = hy + up_x[1]
            hz = hz - up_x[0]
        return hx, hy, hz

    return whole


def edge_body(keep_ref, part_ref, ux_ref, uy_ref, uz_ref, gx_ref, gy_ref, gz_ref):
    nx = part_ref.shape[1]
    lane = lanes(16, 128)
    whole = upper_terms(keep_ref, ux_ref, uy_ref, uz_ref)
    face_z = [jnp.zeros((16, 128), F32), jnp.zeros((16, 128), F32)]
    for i in range(nx):
        hx, hy, hz = whole(part_ref, i)
        if i == nx - 1:
            gx_ref[0] = hy
            gx_ref[1] = hz
        gy_ref[0, i : i + 1, :] = hx[15:16]
        gy_ref[1, i : i + 1, :] = hz[15:16]
        for part, value in enumerate((hx, hy)):
            face_z[part] = jnp.where(lane == i, pltpu.roll(value, i + 1, 1), face_z[part])
    for part in range(2):
        gz_ref[part, 0:16, :] = face_z[part]
        gz_ref[part, 16:24, :] = jnp.zeros((8, 128), F32)


def mag_body(keep_ref, part_ref, ux_ref, uy_ref, uz_ref, out_ref, drive_ref):
    lane, row = lanes(16, 128), rows(16, 128)
    whole = upper_terms(keep_ref, ux_ref, uy_ref, uz_ref)
    hy_x = hz_x = jnp.zeros((16, 128), F32)
    for i in range(part_ref.shape[1]):
        hx, hy, hz = whole(part_ref, i)
        out_ref[0, i] = hx
        out_ref[1, i] = hy
        out_ref[2, i] = hz
        hx_y, hz_y = [jnp.where(row == 0, 0.0, pltpu.roll(v, 1, 0)) for v in (hx, hz)]
        hx_z, hy_z = [jnp.where(lane == 0, 0.0, pltpu.roll(v, 1, 1)) for v in (hx, hy)]
        drive_ref[0, i] = (hz - hz_y) - (hy - hy_z)
        drive_ref[1, i] = (hx - hx_z) - (hz - hz_x)
        drive_ref[2, i] = (hy - hy_x) - (hx - hx_y)
        hy_x, hz_x = hy, hz


def wall_body(decay_ref, gain_ref, poles_ref, e_ref, eps_ref, wall_ref, base_out, slope_out):
    decay = [decay_ref[0:1, p : p + 1] for p in range(poles_ref.shape[0])]
    total = jnp.sum(gain_ref[...], axis=1, keepdims=True)
    for i in range(poles_ref.shape[2]):
        wall = wall_ref[i] == 1
        slope_out[i] = jnp.where(wall, total, 0.5 / eps_ref[i])
        for comp in range(3):
            acc = decay[0] * poles_ref[0, comp, i]
            for p in range(1, poles_ref.shape[0]):
                acc = acc + decay[p] * poles_ref[p, comp, i]
            base_out[comp, i] = jnp.where(wall, acc, e_ref[comp, i])


def elec_body(
    keep_ref, part_ref, dx_ref, dy_ref, dz_ref, base_ref, slope_ref, select_ref, cell_ref, past_ref,
    drive_out, pack_out, cells,
):
    nx = part_ref.shape[1]
    lane = lanes(16, 128)
    row = rows(16, 128)
    dn_x = [dx_ref[part] * keep_ref[3 : 3 + 1, :] for part in range(2)]
    dn_y = [dy_ref[part] * keep_ref[4 : 4 + 1, :] for part in range(2)]
    dn_z = [dz_ref[part, 0:16, :] * keep_ref[5 : 5 + 1, :] for part in range(2)]
    for i in range(nx):
        low = [v if i == 0 else pltpu.roll(v, 128 - i, 1) for v in dn_z]
        hx_z, hy_z = [jnp.where(lane == 0, v, 0.0) for v in low]
        hx_y, hz_y = [jnp.where(row == 0, v[i : i + 1], 0.0) for v in dn_y]
        drive = [
            part_ref[0, i] + (hy_z - hz_y),
            part_ref[1, i] - hx_z,
            part_ref[2, i] + hx_y,
        ]
        if i == 0:
            drive[1] = drive[1] + dn_x[1]
            drive[2] = drive[2] - dn_x[0]
        for comp in range(3):
            drive_out[comp, i] = drive[comp]
        span = pl.ds(i * 16, 16)
        for comp in range(2):
            field = base_ref[comp, i] + slope_ref[i] * drive[comp]
            cells[comp, span, :] = field.astype(BF16)
    packed = past_ref[...] + picked(cells, select_ref[0], cell_ref[0], cell_ref[1])
    packed = packed.astype(BF16)
    pack_out[0] = packed
    pack_out[1] = packed


def picked(cells, select, pick, at):
    lane = lanes(32, 128)
    wide = jnp.zeros((32, 128), F32)
    for e in range(2):
        found = jnp.dot(pick.astype(BF16), cells[e], preferred_element_type=F32)
        value = jnp.sum(found * at, axis=1, keepdims=True)
        wide = jnp.where(lane == 64 * e + 63, value, wide)
    return jnp.dot(select.astype(BF16), wide.astype(BF16), preferred_element_type=F32)


def poles_body(decay_ref, gain_ref, poles_ref, drive_ref, out_ref):
    decay = [decay_ref[0:1, p : p + 1] for p in range(poles_ref.shape[0])]
    gain = [gain_ref[0:1, p : p + 1] for p in range(poles_ref.shape[0])]
    for i in range(poles_ref.shape[2]):
        for comp in range(3):
            drive = drive_ref[comp, i]
            for p in range(poles_ref.shape[0]):
                out_ref[p, comp, i] = decay[p] * poles_ref[p, comp, i] + gain[p] * drive


def field_body(drive_ref, base_ref, slope_ref, h_ref, e_out, h_out):
    h_out[...] = h_ref[...]
    for comp in range(3):
        e_out[comp] = base_ref[comp] + slope_ref[...] * drive_ref[comp]


def pack_body(owner_ref, cell_ref, hist_ref, h_ref, select_out, cell_out, pack_out, cells):
    for comp in range(2):
        for i in range(h_ref.shape[1]):
            cells[comp, i * 16 : (i + 1) * 16, :] = h_ref[comp, i].astype(BF16)
    owner = owner_ref[...]
    onehot = jnp.where(rows(16, 32) == owner, 1.0, 0.0)
    earlier = jnp.where(rows(32, 32) < lanes(32, 32), 1.0, 0.0).astype(BF16)
    count = jnp.dot(onehot.astype(BF16), earlier, preferred_element_type=F32)
    rank = jnp.sum(count * onehot, axis=0, keepdims=True).astype(jnp.int32)
    slot = owner * 8 + rank
    cell = cell_ref[...]
    row = rows(128, 32)
    pick = jnp.where(row == (cell >> 7), 1.0, 0.0).T
    at = jnp.where(row == (cell & 127), 1.0, 0.0).T
    cell_out[0] = pick
    cell_out[1] = at
    packed = jnp.zeros((128, 128), F32)
    for half in range(2):
        select = jnp.where(row == slot + 4 * half, 1.0, 0.0)
        select_out[half] = select
        gap = jnp.zeros((32, 1), F32)
        past = [hist_ref[2 * half + e].astype(F32) for e in range(2)]
        past = jnp.concatenate([past[0], gap, past[1], gap], axis=1)
        packed = packed + jnp.dot(
            select.astype(BF16), past.astype(BF16), preferred_element_type=F32
        )
    pack_out[...] = packed + picked(cells, select, pick, at)


def beside(first, second):
    low = lanes(*first.shape) < 64
    return (
        jnp.where(low, first, pltpu.roll(second, 64, 1)),
        jnp.where(low, pltpu.roll(first, 64, 1), second),
    )


def project_body(core, got_ref, steer_ref, series_out, out_ref):
    got = got_ref[...]
    row, slot = rows(256, 128), lanes(256, 128)
    parts = []
    for half in range(2):
        place = jnp.where(row == (slot >> 2) * 8 + 4 * half + (slot & 3), 1.0, 0.0).astype(BF16)
        moved = dot_t(got, place).astype(BF16)
        parts += [moved[:64], moved[64:]]
    series = jnp.concatenate(parts, axis=1)
    series_out[...] = series
    project_half(1 - core[0], series, steer_ref, out_ref, None)


def project_half(half, series, steer_ref, out_ref, add_ref):
    for n in range(4):
        first = pl.multiple_of(half * 1024 + n * 256, 256)
        part = jnp.dot(series, steer_ref[:, pl.ds(first, 256)], preferred_element_type=F32)
        for m in range(2):
            pair = beside(part[:32, m * 128 : (m + 1) * 128], part[32:, m * 128 : (m + 1) * 128])
            for y in range(2):
                at = 4 * n + 2 * m + y
                out_ref[at] = pair[y] if add_ref is None else pair[y] + add_ref[at]


def project_own_body(core, series_ref, steer_ref, add_ref, out_ref):
    project_half(core[0], series_ref[...], steer_ref, out_ref, add_ref)


def sum_body(got_ref, out_ref):
    total = got_ref[0]
    for a in range(1, got_ref.shape[0]):
        total = total + got_ref[a]
    out_ref[...] = total


def spectrum_body(core, mine_ref, other_ref, table_ref, out_ref):
    mine, other = mine_ref[...], other_ref[...]
    first = core[0] == 0
    both = beside(jnp.where(first, mine, other), jnp.where(first, other, mine))
    both = jnp.concatenate(both, axis=0)
    high = both.astype(BF16)
    low = (both - high.astype(F32)).astype(BF16)
    out_ref[...] = jnp.dot(
        table_ref[core[0]], jnp.concatenate([high, low, high], axis=0), preferred_element_type=F32
    )


def finish_body(got_ref, out_ref):
    total = [got_ref[32 * y : 32 * y + 32, :] for y in range(2)]
    for b in range(1, 4):
        total = [total[y] + got_ref[64 * b + 32 * y : 64 * b + 32 * y + 32, :] for y in range(2)]
    for core, value in enumerate(beside(*total)):
        for g in range(8):
            first = (8 * core + g) * 128
            for s in range(2):
                at = 4 * g + 2 * s
                out_ref[s, :, first : first + 128] = value[at : at + 2]


def spectral_table(steps):
    times = np.arange(steps, dtype=np.float64)
    levels = np.arange(FREQS, dtype=np.float64) + 0.5
    phase = math.pi / (2.0 * FREQS) * levels[:, None] * times[None, :]
    table = np.stack([np.cos(phase), -np.sin(phase)]) / math.sqrt(steps)
    return table.astype(np.float32)


def peer_table(steps):
    table = spectral_table(steps).reshape(2, 8, 2, 8, 2, steps).transpose(2, 3, 1, 0, 4, 5)
    table = table.reshape(2, 256, steps)
    high = table.astype(jnp.bfloat16)
    low = (table - high.astype(np.float32)).astype(jnp.bfloat16)
    return jnp.asarray(np.concatenate([high, high, low], axis=2))


def shift(value, axis, step):
    count = lax.axis_size(axis)
    return lax.ppermute(value, axis, [(i, (i + step) % count) for i in range(count)])


def cross(sender):
    pairs, count = [], lax.axis_size("gxc")
    for g in range(count):
        near = (g + count // 2) % count
        pairs += [(2 * g + sender, 2 * g + 1 - sender), (2 * g + 1 - sender, 2 * near + sender)]
    return pairs


def per_device(
    e_field, h_field, permittivity, wall_mask, poles, pole_decay, pole_gain, face_cells, owners,
    history, steering,
):
    nx, ny, nz = e_field.shape[1:]
    steps = history.shape[0] + 1
    axes = (GX, GY, "gz")
    places = [lax.axis_index(axis) for axis in axes]
    keep = jnp.stack(
        [(at < lax.axis_size(axis) - 1) for at, axis in zip(places, axes)]
        + [at > 0 for at in places]
    ).astype(F32)
    keep = jnp.broadcast_to(keep[:, None], (6, 128))
    core = lax.axis_index("core").reshape(1)
    block = struct(3, nx, ny, nz)
    faces = [struct(2, ny, nz), struct(2, 4 * nx, nz), struct(2, ny + 8, 128)]
    faces_up = [struct(2, ny, nz), struct(2, nx, nz), struct(2, ny + 8, 128)]

    *near, e_near, h_near = call(
        face_body, [*faces, block, block], [HB] * 2, [pltpu.SemaphoreType.DMA((2,))], data=400000
    )(far_off(e_field), far_off(h_field))
    up = [shift(face, axis, -1) for face, axis in zip(near[:2], axes)]
    up.append(lax.ppermute(near[2], ("gxc", "gz"), cross(1)))
    near, e_near, h_near = lax.optimization_barrier((near, e_near, h_near))
    later = [
        poles, permittivity, wall_mask, pole_decay.reshape(1, -1), pole_gain.reshape(1, -1),
        owners.reshape(1, -1), face_cells.reshape(1, -1), jnp.transpose(history, (1, 2, 0)),
    ]
    inner, poles, permittivity, wall_mask, decay, gain, owners, face_cells, history = call(
        inner_body,
        [block, *[struct(*value.shape, dtype=value.dtype) for value in later]],
        [VM] * 2 + [HB] * len(later),
        [pltpu.SemaphoreType.DMA((len(later),))],
        data=2600000,
    )(e_near, h_near, *[far_off(value) for value in later])

    far = call(edge_body, faces_up, [VM] * 5, data=500000)(keep, inner, *up)
    down = [shift(face, axis, 1) for face, axis in zip(far[:2], axes)]
    down.append(lax.ppermute(far[2], ("gxc", "gz"), cross(0)))
    far, owners, poles, inner = lax.optimization_barrier((far, owners, poles, inner))
    h_mid, part = call(mag_body, [block, block], [VM] * 5, data=500000)(keep, inner, *up)
    select, cell, leaving = call(
        pack_body,
        [struct(2, 128, 32), struct(2, 32, 128), struct(128, 128)],
        [VM] * 4,
        scratch=[pltpu.VMEM((2, 128, 128), BF16)],
        data=200000,
    )(owners, face_cells, history, h_mid)
    base, slope = call(wall_body, [block, struct(nx, ny, nz)], [VM] * 6, data=2400000)(
        decay, gain, poles, e_near, permittivity, wall_mask
    )

    drive, leaving = call(
        elec_body,
        [block, struct(2, 128, 128, dtype=BF16)],
        [VM] * 10,
        scratch=[pltpu.VMEM((2, 128, 128), BF16)],
        data=1200000,
    )(keep, part, *down, base, slope, select, cell, leaving)
    arrived = lax.all_to_all(leaving.reshape(32, 8, 128), ("gz", *GX), 0, 0, tiled=True)
    poles_next = call(poles_body, struct(*poles.shape), [VM] * 4, data=3400000)(
        decay, gain, poles, drive
    )
    e_next, h_next = call(field_body, [block, block], [VM] * 4, data=1200000)(
        drive, base, slope, h_mid
    )

    weights = steering.reshape(-1, steering.shape[2])
    series, part = call(
        project_body,
        [struct(64, 512, dtype=BF16), struct(16, 32, 128)],
        [SM] + [VM] * 2,
        flops=1 << 26,
        data=2600000,
    )(core, arrived.reshape(256, 128), weights)
    part = lax.ppermute(part, "core", [(0, 1), (1, 0)])
    series, poles_next = lax.optimization_barrier((series, poles_next))
    part = call(project_own_body, struct(16, 32, 128), [SM] + [VM] * 3, flops=1 << 26, data=2600000)(
        core, series, weights, part
    )
    part = lax.all_to_all(part, ("gxc", "gyl"), 0, 0, tiled=True)
    mine = call(sum_body, struct(32, 128), [VM], data=300000)(part)
    other = lax.ppermute(mine, "core", [(0, 1), (1, 0)])
    core, e_next = lax.optimization_barrier((core, e_next))
    spectra = call(spectrum_body, struct(256, 128), [SM] + [VM] * 3, flops=1 << 27, data=900000)(
        core, mine, other, peer_table(steps)
    )
    spectra = lax.all_to_all(spectra, (*GY, "gxc"), 0, 0, tiled=True)
    far_field = call(finish_body, struct(2, 2, 2048), [VM], data=300000)(spectra)
    return (e_next, h_next, poles_next, far_field)


GX = ("gxc", "core")
GY = ("gyh", "gyl")


def solution(mesh):
    shape = (mesh.shape["gx"] // 2, 2, mesh.shape["gy"] // 2, 2, mesh.shape["gz"])
    mesh = jax.sharding.Mesh(mesh.devices.reshape(shape), (*GX, *GY, "gz"))
    return jax.shard_map(
        per_device,
        mesh=mesh,
        in_specs=(
            P(None, GX, GY, "gz"),
            P(None, GX, GY, "gz"),
            P(GX, GY, "gz"),
            P(GX, GY, "gz"),
            P(None, None, GX, GY, "gz"),
            P(),
            P(),
            P((*GX, *GY, "gz")),
            P((*GX, *GY, "gz"), None),
            P(None, None, (*GX, *GY, "gz")),
            P(None, (*GX, *GY), "gz"),
        ),
        out_specs=(
            P(None, GX, GY, "gz"),
            P(None, GX, GY, "gz"),
            P(None, None, GX, GY, "gz"),
            P(None, (*GX, *GY), "gz"),
        ),
        check_vma=False,
    )
```
